256 devices in a mesh: seq: 32 (over y, x, core), head: 8 (over z).
Axes of the slice: x: 4, y: 4, z: 8, core: 2. Of those that a mesh axis runs over, the one named last changes fastest.
Arguments:
- tokens: bfloat16 [4096, 4096], P('seq'), may hold values from -6 to 6
- key_weight: bfloat16 [4096, 4096], P(None, 'head'), may hold values from -0.09375 to 0.09375
- queries: bfloat16 [4096, 4096], P('seq', 'head'), may hold values from -6 to 6
- values: bfloat16 [4096, 4096], P('seq', 'head'), may hold values from -6 to 6
- grad_out: bfloat16 [4096, 4096], P('seq', 'head'), may hold values from -6 to 6
- inner_start: float32 [32, 128, 128], P('head'), may hold values from -0.5 to 0.5
- head_rate: float32 [32], P('head'), may hold values from 0.01 to 1
Outputs:
- grad_tokens: bfloat16 [4096, 4096], P('seq', 'head')
- grad_key_weight: float32 [4096, 4096], P('seq', 'head')
- grad_query: bfloat16 [4096, 4096], P('seq', 'head')
- grad_value: bfloat16 [4096, 4096], P('seq', 'head')
The draws below stay inside these ranges and needn't reach their ends.
All inputs are finite; a program needn't handle non-finite values.
Results may differ from the reference program's by a relative error of at most 0.029.
Values may be sent and summed in bfloat16 or wider, within the bound.
A program may use at most 128 MiB of HBM per device.

```python
import math
import jax
import jax.numpy as jnp
from jax import lax

D = 4096
HEADS = 32
HEAD = 128
MINI = 16
TOKENS = 4096
N_HEAD = 8


def block_levels(stream_key, extent, split, smallest, top_value):
    factor_of = 1.0
    for dim, parts in split:
        draws = jax.random.uniform(jax.random.fold_in(jax.random.fold_in(stream_key, 6), dim), (parts,), jnp.float32, smallest / len(split), top_value / len(split))
        factor_of = factor_of * jnp.repeat(jnp.exp(draws), extent[dim] // parts).reshape((-1,) + (1,) * (len(extent) - 1 - dim))
    return factor_of


def centred(own_key, dims, scale, reach, pieces=(), held_as=jnp.bfloat16):
    drawn = jax.random.normal(own_key, dims, jnp.float32) * scale
    if len(pieces) > 0:
        drawn = block_levels(own_key, dims, pieces, -0.22, 0.18) * drawn
    return jnp.clip(drawn, min=-reach, max=reach).astype(held_as)


def setup_inputs(seed: int = 0) -> dict:
    key_of = jax.random.split(jax.random.key(seed), 8)
    return {
        "tokens": centred(key_of[0], (TOKENS, D), 1.0, 6.0, ((0, 32),)),
        "key_weight": centred(key_of[1], (D, HEADS * HEAD), D ** -0.5, 0.09375, ((1, 8),)),
        "queries": centred(key_of[2], (TOKENS, HEADS * HEAD), 1.0, 6.0, ((0, 32), (1, 8))),
        "values": centred(key_of[3], (TOKENS, HEADS * HEAD), 1.0, 6.0, ((0, 32), (1, 8))),
        "grad_out": centred(key_of[4], (TOKENS, HEADS * HEAD), 1.0, 6.0, ((0, 32), (1, 8))),
        "inner_start": centred(key_of[5], (HEADS, HEAD, HEAD), HEAD ** -0.5, 0.5, ((0, 8),), jnp.float32),
        "head_rate": jnp.clip(jnp.exp(math.log(1.0) - 4.6051702 * jax.random.uniform(key_of[6], (HEADS,), jnp.float32) ** block_levels(key_of[6], (HEADS,), ((0, 8),), -0.2, 0.2)), 0.01, 1.0),
    }


rate_base = 0.1
norm_eps = 1e-06
best = lax.Precision.HIGHEST

def matmul(left, right):
    return jnp.dot(left, right, precision=best, preferred_element_type=jnp.float32)

def one_head(packed):
    keys, value_rows, query_rows, grad_rows, start, rate_one = packed
    rate = rate_base * rate_one

    def forward(state, batch):
        keys_b, value_b = batch
        resid = matmul(keys_b, state) - value_b
        new = state - rate * matmul(keys_b.T, resid)
        return (new, (state, new))
    _, (before, after) = lax.scan(forward, start, (keys, value_rows))
    grad_query = jnp.einsum('tbj,tij->tbi', grad_rows, after, precision=best)

    def backward(carry, batch):
        keys_b, value_b, query_b, grad_b, state = batch
        adjoint = carry + matmul(query_b.T, grad_b)
        resid = matmul(keys_b, state) - value_b
        keyed = matmul(keys_b, adjoint)
        key_adj = -rate * (matmul(resid, adjoint.T) + matmul(keyed, state.T))
        return (adjoint - rate * matmul(keys_b.T, keyed), (key_adj, rate * keyed))
    _, (key_adj, grad_value) = lax.scan(backward, jnp.zeros_like(start), (keys, value_rows, query_rows, grad_rows, before), reverse=True)
    return (grad_query, key_adj, grad_value)

def reference(tokens, key_weight, queries, values, grad_out, inner_start, head_rate):
    batches = TOKENS // MINI
    shape4 = (batches, MINI, HEADS, HEAD)
    keys_raw = jnp.dot(tokens, key_weight, preferred_element_type=jnp.float32).reshape(shape4)
    inv_norm = lax.rsqrt(lax.optimization_barrier(jnp.sum(keys_raw * keys_raw, axis=-1, keepdims=True)) + norm_eps)
    keys = keys_raw * inv_norm

    def heads_first(array):
        return jnp.transpose(array.astype(jnp.float32).reshape(shape4), (2, 0, 1, 3))
    grad_query, key_adj, grad_value = lax.map(one_head, (heads_first(keys), heads_first(values), heads_first(queries), heads_first(grad_out), inner_start, head_rate))

    def rows_back(array):
        return jnp.transpose(array, (1, 2, 0, 3))
    key_adj = rows_back(key_adj)
    along = lax.optimization_barrier(jnp.sum(keys * key_adj, axis=-1, keepdims=True))
    raw_adj = ((key_adj - keys * along) * inv_norm).astype(jnp.bfloat16).reshape(TOKENS, HEADS * HEAD)
    grad_key_weight = lax.dot_general(tokens, raw_adj, (((0,), (0,)), ((), ())), preferred_element_type=jnp.float32)
    columns = HEADS * HEAD // N_HEAD
    total = jnp.zeros((TOKENS, D), jnp.float32)
    for group in range(N_HEAD):
        part = lax.dot_general(raw_adj[:, group * columns:(group + 1) * columns], key_weight[:, group * columns:(group + 1) * columns], (((1,), (1,)), ((), ())), preferred_element_type=jnp.float32)
        total = total + part.astype(jnp.bfloat16).astype(jnp.float32)
    grad_tokens = total.astype(jnp.bfloat16)
    grad_query = rows_back(grad_query).reshape(TOKENS, HEADS * HEAD).astype(jnp.bfloat16)
    grad_value = rows_back(grad_value).reshape(TOKENS, HEADS * HEAD).astype(jnp.bfloat16)
    return (grad_tokens, grad_key_weight, grad_query, grad_value)
```

```python
import jax
import jax.numpy as jnp
from jax import lax
from jax.experimental import pallas as pl
from jax.experimental.pallas import tpu as pltpu
from jax.sharding import PartitionSpec as P

MESH = pl.DeviceIdType.MESH
bf16 = jnp.bfloat16
f32 = jnp.float32
rate_base = 0.1
norm_eps = 1e-06
W = 128
NH = 4
NX, NY, NC = 4, 4, 2
ROW = NX * NC
NS = ROW * NY
NZ = 8


def mm(a, b):
    return lax.dot_general(a, b, (((1,), (0,)), ((), ())), preferred_element_type=f32)


def nt(a, b):
    return lax.dot_general(a, b, (((1,), (1,)), ((), ())), preferred_element_type=f32)


def tn(a, b):
    return lax.dot_general(a, b, (((0,), (0,)), ((), ())), preferred_element_type=f32)


def batch_of():
    rows = lax.broadcasted_iota(jnp.int32, (W, W), 0) >> 4
    cols = lax.broadcasted_iota(jnp.int32, (W, W), 1) >> 4
    return rows, cols


def local_maps(kraw, v, q, g, r):
    bi, bj = batch_of()
    inv = lax.rsqrt(jnp.sum(kraw * kraw, axis=1, keepdims=True) + norm_eps)
    k = kraw * inv
    kb = k.astype(bf16)
    m = r * nt(kb, kb)
    x1 = jnp.where(((bi >> 1) == (bj >> 1)) & (bi > bj), m, 0.0)
    x2 = jnp.where(((bi >> 2) == (bj >> 2)) & ((bi >> 1) > (bj >> 1)), m, 0.0)
    x3 = jnp.where((bi >> 2) > (bj >> 2), m, 0.0)
    rows = lax.broadcasted_iota(jnp.int32, (W, W), 0)
    cols = lax.broadcasted_iota(jnp.int32, (W, W), 1)
    t1 = jnp.where(rows == cols, 1.0, 0.0) - x1
    t1b = t1.astype(bf16)
    t2 = t1 - mm(mm(t1b, x2.astype(bf16)).astype(bf16), t1b)
    t2b = t2.astype(bf16)
    t3 = t2 - mm(mm(t2b, x3.astype(bf16)).astype(bf16), t2b)
    tb = t3.astype(bf16)
    tk = mm(tb, kb).astype(bf16)
    tv = mm(tb, v)
    z = mm(jnp.where(bi <= bj, nt(kb, q), 0.0).astype(bf16), g).astype(bf16)
    ttk = tn(tb, kb).astype(bf16)
    ttz = tn(tb, z)
    e0 = (-r * tn(tk, kb)).astype(bf16)
    f0 = (r * tn(tv.astype(bf16), kb)).astype(bf16)
    e1 = (-r * tn(kb, tk)).astype(bf16)
    f1 = (tn(g, q) - r * tn(ttz.astype(bf16), kb)).astype(bf16)
    return k, inv, kb, tk, tv, ttk, ttz, e0, f0, e1, f1


def join(a, b):
    return a.astype(f32) + b.astype(f32) + mm(a.astype(bf16), b[:W].astype(bf16))


def apply(state, m):
    return state + mm(state.astype(bf16), m[:W].astype(bf16)) + m[W:].astype(f32)


def kernel(
    tok_ref, kw_ref, q_ref, v_ref, g_ref, w0_ref, rate_ref,
    gt_ref, gkw_ref, gq_ref, gv_ref,
    tokcol, tok_t, ef_send, ef_recv, tot_send, tot_recv, nodes, state, x_send, wl,
    kf, invf, kbs, tks, tvs, ttks, ttzs, ubs, raw_all, part, zrecv,
    tok_ss, tok_rs, ef_ss, ef_rs, tot_ss, tot_rs, x_ss, wl_rs, ag_ss, ag_rs, z_ss, z_rs,
):
    me = lax.axis_index("seq")
    zme = lax.axis_index("head")
    y = me // ROW
    p = me % ROW
    x = p // NC
    core = p % NC
    row0 = y * ROW
    sib = me + 1 - 2 * core

    def seq_copy(src, dst, ss, rs, to):
        return pltpu.make_async_remote_copy(
            src_ref=src, dst_ref=dst, send_sem=ss, recv_sem=rs,
            device_id={"seq": to}, device_id_type=MESH,
        )

    def head_copy(src, dst, ss, rs, to):
        return pltpu.make_async_remote_copy(
            src_ref=src, dst_ref=dst, send_sem=ss, recv_sem=rs,
            device_id={"head": to}, device_id_type=MESH,
        )

    barrier = pltpu.get_barrier_semaphore()

    def greet_seq(off, c):
        pl.semaphore_signal(
            barrier, inc=1, device_id={"seq": (me + off) % NS}, device_id_type=MESH
        )
        return c

    def greet_head(off, c):
        pl.semaphore_signal(
            barrier, inc=1, device_id={"head": (zme + off) % NZ}, device_id_type=MESH
        )
        return c

    lax.fori_loop(1, NS, greet_seq, 0)
    lax.fori_loop(1, NZ, greet_head, 0)
    pl.semaphore_wait(barrier, NS - 1 + NZ - 1)

    def tok_copy(off):
        to = (me + off) % NS
        cols = pl.ds(pl.multiple_of(to * W, W), W)
        return seq_copy(tok_ref.at[:, cols], tokcol.at[me], tok_ss.at[off], tok_rs.at[off], to)

    def tok_start(off, c):
        tok_copy(off).start()
        return c

    lax.fori_loop(1, NS, tok_start, 0)

    kraw = mm(tok_ref[...], kw_ref[...])
    rates = [rate_base * rate_ref[h] for h in range(NH)]
    for h in range(NH):
        hs = slice(h * W, h * W + W)
        k, inv, kb, tk, tv, ttk, ttz, e0, f0, e1, f1 = local_maps(
            kraw[:, hs], v_ref[:, hs], q_ref[:, hs], g_ref[:, hs], rates[h]
        )
        kf[h] = k
        invf[h] = jnp.broadcast_to(inv, (W, W))
        kbs[h] = kb
        tks[h] = tk
        tvs[h] = tv
        ttks[h] = ttk
        ttzs[h] = ttz
        ef_send[0, h, :W] = e0
        ef_send[0, h, W:] = f0
        ef_send[1, h, :W] = e1
        ef_send[1, h, W:] = f1
        for role in range(2):
            slot = p if role == 0 else ROW - 1 - p
            here = NC * h + role

            @pl.when(p != here)
            def _():
                seq_copy(
                    ef_send.at[role, h], ef_recv.at[slot], ef_ss.at[role, h],
                    ef_rs.at[slot], row0 + here,
                ).start()

            @pl.when(p == here)
            def _():
                ef_recv[slot] = ef_send[role, h]

    own_slot = jnp.where(core == 0, p, ROW - 1 - p)
    for slot in range(ROW):
        frm = jnp.where(core == 0, slot, ROW - 1 - slot)

        @pl.when(slot != own_slot)
        def _():
            seq_copy(
                ef_send.at[0, 0], ef_recv.at[slot], ef_ss.at[0, 0], ef_rs.at[slot], row0 + frm
            ).wait_recv()

    for i in range(4):
        nodes[i] = join(ef_recv[2 * i], ef_recv[2 * i + 1])
    for i in range(2):
        nodes[4 + i] = join(nodes[2 * i], nodes[2 * i + 1])
    tot_send[...] = join(nodes[4], nodes[5]).astype(bf16)

    pos = jnp.where(core == 0, y, NY - 1 - y)
    for to_pos in range(1, NY):
        to_y = jnp.where(core == 0, to_pos, NY - 1 - to_pos)

        @pl.when(to_pos > pos)
        def _():
            seq_copy(
                tot_send, tot_recv.at[pos], tot_ss.at[to_pos], tot_rs.at[pos], to_y * ROW + p
            ).start()

    cols = pl.ds(pl.multiple_of(me * W, W), W)
    tokcol[me] = tok_ref[:, cols]

    def tok_wait(off, c):
        frm = (me + NS - off) % NS
        seq_copy(
            tokcol.at[frm], tokcol.at[frm], tok_ss.at[off], tok_rs.at[off], frm
        ).wait_recv()
        return c

    lax.fori_loop(1, NS, tok_wait, 0)

    def turn(s, c):
        tok_t[:, pl.ds(pl.multiple_of(s * W, W), W)] = tokcol[s].T
        return c

    lax.fori_loop(0, NS, turn, 0)

    state[...] = jnp.where(core == 0, w0_ref[x].T, 0.0)
    for j in range(NY - 1):
        frm_y = jnp.where(core == 0, j, NY - 1 - j)

        @pl.when(j < pos)
        def _():
            seq_copy(
                tot_send, tot_recv.at[j], tot_ss.at[0], tot_rs.at[j], frm_y * ROW + p
            ).wait_recv()
            state[...] = apply(state[...], tot_recv[j])

    xs = [None] * ROW
    xs[0] = state[...]
    xs[4] = apply(xs[0], nodes[4])
    xs[2] = apply(xs[0], nodes[0])
    xs[6] = apply(xs[4], nodes[2])
    for i in (0, 2, 4, 6):
        xs[i + 1] = apply(xs[i], ef_recv[i])
    for slot in range(ROW):
        x_send[slot] = xs[slot].astype(bf16)
        to = jnp.where(core == 0, slot, ROW - 1 - slot)

        @pl.when(to != p)
        def _():
            seq_copy(
                x_send.at[slot], wl.at[x, core], x_ss.at[slot], wl_rs.at[x, core], row0 + to
            ).start()

        @pl.when(to == p)
        def _():
            wl[x, core] = x_send[slot]

    def shard(yy, xx, cc):
        return (yy * NX + xx) * NC + cc

    def peer(axis, i):
        if axis == 0:
            return shard(y, (x + i) % NX, core)
        return shard((y + i) % NY, x, core)

    def ag_copy(half, s, sem, to):
        return seq_copy(
            raw_all.at[half, s], raw_all.at[half, s], ag_ss.at[half, sem], ag_rs.at[half, s], to
        )

    for half in range(2):
        for h in (2 * half, 2 * half + 1):
            hs = slice(h * W, h * W + W)
            for role in range(2):
                @pl.when(p != NC * h + role)
                def _():
                    seq_copy(
                        x_send.at[0], wl.at[h, role], x_ss.at[0], wl_rs.at[h, role],
                        row0 + NC * h + role,
                    ).wait_recv()

            bi, bj = batch_of()
            r = rates[h]
            w, l = wl[h, 0], wl[h, 1]
            q, g, kb = q_ref[:, hs], g_ref[:, hs], kbs[h]
            ub = (nt(tks[h], w) - tvs[h]).astype(bf16)
            yy = nt(ttks[h], l) + ttzs[h]
            yb = yy.astype(bf16)
            gv_ref[:, hs] = (r * yy).astype(bf16)
            ubs[h] = ub
            pm = jnp.where(bi <= bj, nt(ub, g), 0.0).astype(bf16)
            sm = (
                jnp.where(bi < bj, nt(ub, yb), 0.0) + jnp.where(bi > bj, nt(yb, ub), 0.0)
            ).astype(bf16)
            ka = -r * (mm(ub, l) + mm(yb, w) + mm(pm, q) - r * mm(sm, kb))
            k = kf[h]
            along = jnp.sum(k * ka, axis=1, keepdims=True)
            raw_all[half, me, :, (h % 2) * W:(h % 2) * W + W] = (
                (ka - k * along) * invf[h]
            ).astype(bf16)
        for i in range(1, 4):
            ag_copy(half, me, i, peer(half, i)).start()
        ag_copy(half, me, 16, sib).start()

    raw = jnp.concatenate([raw_all[0, me], raw_all[1, me]], axis=1)

    def z_copy(off):
        return head_copy(part.at[off], zrecv.at[off], z_ss.at[off], z_rs.at[off], (zme + off) % NZ)

    for off in (4, 3, 5, 2, 6, 1, 7, 0):
        to = (zme + off) % NZ
        rows = pl.ds(pl.multiple_of(to * NH * W, NH * W), NH * W)
        part[off] = nt(raw, kw_ref[rows, :]).astype(bf16)
        if off:
            z_copy(off).start()

    for half in range(2):
        for j in range(4):
            s = me if j == 0 else peer(half, j)
            if j:
                ag_copy(half, s, 0, sib).wait_recv()
                ag_copy(half, s, 16 + j, sib).start()
            for i in range(1, 4):
                ag_copy(half, s, 3 + 3 * j + i, peer(1 - half, i)).start()

    for h in range(NH):
        hs = slice(h * W, h * W + W)
        bi, bj = batch_of()
        g = g_ref[:, hs]
        low = jnp.where(bi >= bj, nt(g, ubs[h]), 0.0).astype(bf16)
        gq_ref[:, hs] = (mm(g, wl[h, 0]) - rates[h] * mm(low, kbs[h])).astype(bf16)

    for half in range(2):
        for j in range(4):
            for i in range(1, 4):
                if half == 0:
                    s = shard((y + i) % NY, (x + j) % NX, core)
                else:
                    s = shard((y + j) % NY, (x + i) % NX, core)
                ag_copy(half, s, 0, sib).wait_recv()
                ag_copy(half, s, 16 + 4 * i + j, sib).start()

    acc = part[0].astype(f32)
    for off in (1, 7, 2, 6, 3, 5, 4):
        z_copy(off).wait_recv()
        acc = acc + zrecv[off].astype(f32)
    gt_ref[...] = acc.astype(bf16)

    for half in range(2):
        def sib_wait(i, c, half=half):
            ag_copy(half, NC * i + 1 - core, 0, sib).wait_recv()
            return c

        lax.fori_loop(0, NS // NC, sib_wait, 0)
        gkw_ref[:, 2 * W * half:2 * W * (half + 1)] = mm(
            tok_t[...], raw_all[half].reshape(NS * W, 2 * W)
        )

    def tok_sent(off, c):
        tok_copy(off).wait_send()
        return c

    lax.fori_loop(1, NS, tok_sent, 0)
    for h in range(NH):
        for role in range(2):
            @pl.when(p != NC * h + role)
            def _():
                seq_copy(
                    ef_send.at[role, h], ef_recv.at[0], ef_ss.at[role, h], ef_rs.at[0], sib
                ).wait_send()
    for to_pos in range(1, NY):
        @pl.when(to_pos > pos)
        def _():
            seq_copy(tot_send, tot_recv.at[0], tot_ss.at[to_pos], tot_rs.at[0], sib).wait_send()
    for slot in range(ROW):
        @pl.when(slot != own_slot)
        def _():
            seq_copy(
                x_send.at[slot], wl.at[0, 0], x_ss.at[slot], wl_rs.at[0, 0], sib
            ).wait_send()
    for half in range(2):
        def ag_sent(i, c, half=half):
            ag_copy(half, me, i, sib).wait_send()
            return c

        lax.fori_loop(1, 32, ag_sent, 0)
    for off in range(1, NZ):
        z_copy(off).wait_send()


def per_device(tokens, key_weight, queries, values, grad_out, inner_start, head_rate):
    vmem = pl.BlockSpec(memory_space=pltpu.VMEM)
    smem = pl.BlockSpec(memory_space=pltpu.SMEM)
    cols = NH * W
    sem = pltpu.SemaphoreType.DMA
    return pl.pallas_call(
        kernel,
        out_shape=(
            jax.ShapeDtypeStruct((W, cols), bf16),
            jax.ShapeDtypeStruct((W, cols), f32),
            jax.ShapeDtypeStruct((W, cols), bf16),
            jax.ShapeDtypeStruct((W, cols), bf16),
        ),
        in_specs=[vmem] * 6 + [smem],
        out_specs=(vmem,) * 4,
        scratch_shapes=[
            pltpu.VMEM((NS, W, W), bf16),
            pltpu.VMEM((W, NS * W), bf16),
            pltpu.VMEM((2, NH, 2 * W, W), bf16),
            pltpu.VMEM((ROW, 2 * W, W), bf16),
            pltpu.VMEM((2 * W, W), bf16),
            pltpu.VMEM((NY, 2 * W, W), bf16),
            pltpu.VMEM((6, 2 * W, W), f32),
            pltpu.VMEM((W, W), f32),
            pltpu.VMEM((ROW, W, W), bf16),
            pltpu.VMEM((NH, 2, W, W), bf16),
            pltpu.VMEM((NH, W, W), f32),
            pltpu.VMEM((NH, W, W), f32),
            pltpu.VMEM((NH, W, W), bf16),
            pltpu.VMEM((NH, W, W), bf16),
            pltpu.VMEM((NH, W, W), f32),
            pltpu.VMEM((NH, W, W), bf16),
            pltpu.VMEM((NH, W, W), f32),
            pltpu.VMEM((NH, W, W), bf16),
            pltpu.VMEM((2, NS, W, 2 * W), bf16),
            pltpu.VMEM((NZ, W, cols), bf16),
            pltpu.VMEM((NZ, W, cols), bf16),
            sem((NS,)), sem((NS,)),
            sem((2, NH)), sem((ROW,)),
            sem((NY,)), sem((NY,)),
            sem((ROW,)), sem((NH, 2)),
            sem((2, NS)), sem((2, NS)),
            sem((NZ,)), sem((NZ,)),
        ],
        compiler_params=pltpu.CompilerParams(
            collective_id=0, has_side_effects=True, vmem_limit_bytes=48 * 1024 * 1024
        ),
        name="layer",
    )(tokens, key_weight, queries, values, grad_out, inner_start, head_rate)


def solution(mesh):
    placed = (
        P("seq", None),
        P(None, "head"),
        P("seq", "head"),
        P("seq", "head"),
        P("seq", "head"),
        P("head", None, None),
        P("head"),
    )
    return jax.shard_map(
        per_device,
        mesh=mesh,
        in_specs=placed,
        out_specs=(P("seq", "head"),) * 4,
        check_vma=False,
    )
```

```python
import jax
import jax.numpy as jnp
from jax import lax
from jax.experimental import pallas as pl
from jax.experimental.pallas import tpu as pltpu
from jax.sharding import PartitionSpec as P

MESH = pl.DeviceIdType.MESH
bf16 = jnp.bfloat16
f32 = jnp.float32
rate_base = 0.1
norm_eps = 1e-06
W = 128
NH = 4
NX, NY, NC = 4, 4, 2
ROW = NX * NC
NS = ROW * NY
NZ = 8
TZ = W // NZ
KW_PARTS = 4


def mm(a, b):
    return lax.dot_general(a, b, (((1,), (0,)), ((), ())), preferred_element_type=f32)


def nt(a, b):
    return lax.dot_general(a, b, (((1,), (1,)), ((), ())), preferred_element_type=f32)


def tn(a, b):
    return lax.dot_general(a, b, (((0,), (0,)), ((), ())), preferred_element_type=f32)


def batch_of():
    rows = lax.broadcasted_iota(jnp.int32, (W, W), 0) >> 4
    cols = lax.broadcasted_iota(jnp.int32, (W, W), 1) >> 4
    return rows, cols


def local_maps(kraw, v, q, g, r):
    bi, bj = batch_of()
    inv = lax.rsqrt(jnp.sum(kraw * kraw, axis=1, keepdims=True) + norm_eps)
    k = kraw * inv
    kb = k.astype(bf16)
    m = r * nt(kb, kb)
    x1 = jnp.where(((bi >> 1) == (bj >> 1)) & (bi > bj), m, 0.0)
    x2 = jnp.where(((bi >> 2) == (bj >> 2)) & ((bi >> 1) > (bj >> 1)), m, 0.0)
    x3 = jnp.where((bi >> 2) > (bj >> 2), m, 0.0)
    rows = lax.broadcasted_iota(jnp.int32, (W, W), 0)
    cols = lax.broadcasted_iota(jnp.int32, (W, W), 1)
    t1 = jnp.where(rows == cols, 1.0, 0.0) - x1
    t1b = t1.astype(bf16)
    t2 = t1 - mm(mm(t1b, x2.astype(bf16)).astype(bf16), t1b)
    t2b = t2.astype(bf16)
    t3 = t2 - mm(mm(t2b, x3.astype(bf16)).astype(bf16), t2b)
    tb = t3.astype(bf16)
    tk = mm(tb, kb).astype(bf16)
    tv = mm(tb, v)
    z = mm(jnp.where(bi <= bj, nt(kb, q), 0.0).astype(bf16), g).astype(bf16)
    ttk = tn(tb, kb).astype(bf16)
    ttz = tn(tb, z)
    e0 = (-r * tn(tk, kb)).astype(bf16)
    f0 = (r * tn(tv.astype(bf16), kb)).astype(bf16)
    e1 = (-r * tn(kb, tk)).astype(bf16)
    f1 = (tn(g, q) - r * tn(ttz.astype(bf16), kb)).astype(bf16)
    return k, inv, kb, tk, tv, ttk, ttz, e0, f0, e1, f1


def join(a, b):
    return a.astype(f32) + b.astype(f32) + mm(a.astype(bf16), b[:W].astype(bf16))


def apply(state, m):
    return state + mm(state.astype(bf16), m[:W].astype(bf16)) + m[W:].astype(f32)


def kernel(
    tok_hbm, kw_hbm, q_hbm, v_hbm, g_hbm, w0_hbm, rate_ref,
    gt_ref, gkw_ref, gq_ref, gv_ref,
    tok_ref, kw_ref, q_ref, v_ref, g_ref, w0_ref,
    tokcol, tok_t, ef_send, ef_recv, tot_send, tot_recv, nodes, state, x_send, wl,
    kf, invf, kbs, tks, tvs, ttks, ttzs, ubs, raw_all, zs, zr,
    in_s, tok_ss, tok_rs, tz_ss, tz_rs, ef_ss, ef_rs, tot_ss, tot_rs, x_ss, x_rs,
    ag_ss, ag_rs, sib_rs, z_ss, z_rs,
):
    me = lax.axis_index("seq")
    zme = lax.axis_index("head")
    y = me // ROW
    p = me % ROW
    x = p // NC
    core = p % NC
    row0 = y * ROW
    sib = me + 1 - 2 * core

    def seq_copy(src, dst, ss, rs, to):
        return pltpu.make_async_remote_copy(
            src_ref=src, dst_ref=dst, send_sem=ss, recv_sem=rs,
            device_id={"seq": to}, device_id_type=MESH,
        )

    def head_copy(src, dst, ss, rs, to):
        return pltpu.make_async_remote_copy(
            src_ref=src, dst_ref=dst, send_sem=ss, recv_sem=rs,
            device_id={"head": to}, device_id_type=MESH,
        )

    deep = kw_ref.shape[0] // KW_PARTS
    loads = [pltpu.make_async_copy(tok_hbm, tok_ref, in_s.at[0])]
    for i in range(KW_PARTS):
        rows = pl.ds(i * deep, deep)
        loads.append(pltpu.make_async_copy(kw_hbm.at[rows], kw_ref.at[rows], in_s.at[1 + i]))
    for i, (src, dst) in enumerate(
        ((q_hbm, q_ref), (v_hbm, v_ref), (g_hbm, g_ref), (w0_hbm, w0_ref))
    ):
        loads.append(pltpu.make_async_copy(src, dst, in_s.at[1 + KW_PARTS + i]))
    for load in loads:
        load.start()

    barrier = pltpu.get_barrier_semaphore()

    def greet_seq(off, c):
        pl.semaphore_signal(
            barrier, inc=1, device_id={"seq": (me + off) % NS}, device_id_type=MESH
        )
        return c

    lax.fori_loop(1, NS, greet_seq, 0)
    up, down = (zme + 1) % NZ, (zme + NZ - 1) % NZ
    for to in (up, down):
        pl.semaphore_signal(barrier, inc=1, device_id={"head": to}, device_id_type=MESH)

    loads[0].wait()
    kraw = None
    for i in range(KW_PARTS):
        loads[1 + i].wait()
        rows = slice(i * deep, (i + 1) * deep)
        prod = mm(tok_ref[:, rows], kw_ref[rows, :])
        kraw = prod if kraw is None else kraw + prod
    for load in loads[1 + KW_PARTS:]:
        load.wait()
    rates = [rate_base * rate_ref[h] for h in range(NH)]
    for h in range(NH):
        hs = slice(h * W, h * W + W)
        k, inv, kb, tk, tv, ttk, ttz, e0, f0, e1, f1 = local_maps(
            kraw[:, hs], v_ref[:, hs], q_ref[:, hs], g_ref[:, hs], rates[h]
        )
        kf[h] = k
        invf[h] = jnp.broadcast_to(inv, (W, W))
        kbs[h] = kb
        tks[h] = tk
        tvs[h] = tv
        ttks[h] = ttk
        ttzs[h] = ttz
        ef_send[0, h, :W] = e0
        ef_send[0, h, W:] = f0
        ef_send[1, h, :W] = e1
        ef_send[1, h, W:] = f1
        if h == 0:
            pl.semaphore_wait(barrier, NS - 1 + 2)
        for role in range(2):
            slot = p if role == 0 else ROW - 1 - p
            here = NC * h + role

            @pl.when(p != here)
            def _():
                seq_copy(
                    ef_send.at[role, h], ef_recv.at[slot], ef_ss, ef_rs, row0 + here
                ).start()

            @pl.when(p == here)
            def _():
                ef_recv[slot] = ef_send[role, h]

    my_slot = (core * NY + y) * NX + x
    part_rows = pl.ds(pl.multiple_of(zme * TZ, TZ), TZ)

    def tok_start(off, c):
        to = (me + off) % NS
        cols = pl.ds(pl.multiple_of(to * W, W), W)
        seq_copy(
            tok_ref.at[part_rows, cols], tokcol.at[zme, my_slot], tok_ss, tok_rs, to
        ).start()
        return c

    lax.fori_loop(1, NS, tok_start, 0)
    tokcol[zme, my_slot] = tok_ref[part_rows, pl.ds(pl.multiple_of(me * W, W), W)]
    tok_all = tokcol.at[0, pl.ds(0, NS - 1)]
    tok_sum = seq_copy(tok_all, tok_all, tok_ss, tok_rs, sib)

    def tz(dist, way, wait=False):
        blk = (zme + NZ - way * dist) % NZ
        ref = tokcol.at[blk]
        if dist == 3:
            ref = tokcol.at[blk, pl.ds(0 if way == 1 else NS // 2, NS // 2)]
        sem = tz_rs.at[2 * dist + (way == 1)]
        return head_copy(ref, ref, tz_ss, sem, up if way == 1 else down)

    def tz_arrived(dist, way):
        blk = (zme + NZ - way * dist) % NZ
        ref = tokcol.at[blk]
        if dist == 4:
            ref = tokcol.at[blk, pl.ds(0 if way == 1 else NS // 2, NS // 2)]
        sem = tz_rs.at[2 * (dist - 1) + (way == 1)]
        head_copy(ref, ref, tz_ss, sem, up).wait_recv()

    own_slot = jnp.where(core == 0, p, ROW - 1 - p)
    some = ef_recv.at[pl.ds(0, ROW - 1)]
    ef_sum = seq_copy(some, some, ef_ss, ef_rs, sib)
    ef_sum.wait_recv()
    for i in range(4):
        nodes[i] = join(ef_recv[2 * i], ef_recv[2 * i + 1])
    for i in range(2):
        nodes[4 + i] = join(nodes[2 * i], nodes[2 * i + 1])
    tot_send[...] = join(nodes[4], nodes[5]).astype(bf16)

    pos = jnp.where(core == 0, y, NY - 1 - y)
    for to_pos in range(1, NY):
        to_y = jnp.where(core == 0, to_pos, NY - 1 - to_pos)

        @pl.when(to_pos > pos)
        def _():
            seq_copy(
                tot_send, tot_recv.at[pos], tot_ss.at[to_pos], tot_rs.at[pos], to_y * ROW + p
            ).start()

    tok_sum.wait_recv()
    tz(0, 1).start()
    tz(0, -1).start()

    state[...] = jnp.where(core == 0, w0_ref[x].T, 0.0)
    for j in range(NY - 1):
        frm_y = jnp.where(core == 0, j, NY - 1 - j)

        @pl.when(j < pos)
        def _():
            seq_copy(
                tot_send, tot_recv.at[j], tot_ss.at[0], tot_rs.at[j], frm_y * ROW + p
            ).wait_recv()
            state[...] = apply(state[...], tot_recv[j])

    xs = [None] * ROW
    xs[0] = state[...]
    xs[4] = apply(xs[0], nodes[4])
    xs[2] = apply(xs[0], nodes[0])
    xs[6] = apply(xs[4], nodes[2])
    for i in (0, 2, 4, 6):
        xs[i + 1] = apply(xs[i], ef_recv[i])
    for slot in range(ROW):
        x_send[slot] = xs[slot].astype(bf16)
        to = jnp.where(core == 0, slot, ROW - 1 - slot)

        @pl.when(to != p)
        def _():
            seq_copy(x_send.at[slot], wl.at[2 * x + core], x_ss, x_rs, row0 + to).start()

        @pl.when(to == p)
        def _():
            wl[2 * x + core] = x_send[slot]

    for way in (1, -1):
        tz_arrived(1, way)
        tz(1, way).start()
    some_x = wl.at[pl.ds(0, ROW - 1)]
    x_sum = seq_copy(some_x, some_x, x_ss, x_rs, sib)
    x_sum.wait_recv()

    mine = ((x, y), (y, x))

    def spot(half, da, db):
        a, b = mine[half]
        return core * 4 + (b + db) % 4, (a + da) % 4

    def device(half, da, db):
        a, b = mine[half]
        a, b = (a + da) % 4, (b + db) % 4
        xx, yy = (a, b) if half == 0 else (b, a)
        return (yy * NX + xx) * NC + core

    def shard(half, da, db, piece=None):
        g, a = spot(half, da, db)
        if piece is None:
            return raw_all.at[half, g, a]
        return raw_all.at[half, g, a, pl.ds(piece * (W // 2), W // 2)]

    def ag_sem(half, da, kind):
        return ag_rs.at[half, 4 * (da % 4) + kind]

    def ag_send(half, da, db, leg, way, piece=None):
        ref = shard(half, da, db, piece)
        to = device(half, way, 0) if leg == 0 else device(half, 0, way)
        kind = (0 if way == 1 else 1) if piece is None else 2 + piece
        sem = ag_rs.at[half, 16 + kind] if leg == 0 else ag_sem(half, da, kind)
        seq_copy(ref, ref, ag_ss.at[half], sem, to).start()

    def ag_wait(half, da, db, leg, kind):
        ref = shard(half, da, db, kind - 2 if kind >= 2 else None)
        sem = ag_rs.at[half, 16 + kind] if leg == 0 else ag_sem(half, da, kind)
        seq_copy(ref, ref, ag_ss.at[half], sem, sib).wait_recv()

    def first_leg_on(half):
        ag_wait(half, -1, 0, 0, 0)
        ag_send(half, -1, 0, 0, 1, 0)
        ag_wait(half, 1, 0, 0, 1)
        ag_send(half, 1, 0, 0, -1, 1)

    def second_leg(half, da):
        ag_send(half, da, 0, 1, 1)
        ag_send(half, da, 0, 1, -1)

    def second_leg_on(half, da):
        ag_wait(half, da, -1, 1, 0)
        ag_send(half, da, -1, 1, 1, 0)
        ag_wait(half, da, 1, 1, 1)
        ag_send(half, da, 1, 1, -1, 1)

    def sib_copy(half, db, cc):
        b = mine[half][1]
        ref = raw_all.at[half, cc * 4 + (b + db) % 4]
        return seq_copy(ref, ref, ag_ss.at[half], sib_rs.at[half, db % 4], sib)

    for half in range(2):
        raws = []
        for h in (2 * half, 2 * half + 1):
            hs = slice(h * W, h * W + W)
            bi, bj = batch_of()
            r = rates[h]
            w, l = wl[2 * h], wl[2 * h + 1]
            q, g, kb = q_ref[:, hs], g_ref[:, hs], kbs[h]
            ub = (nt(tks[h], w) - tvs[h]).astype(bf16)
            yy = nt(ttks[h], l) + ttzs[h]
            yb = yy.astype(bf16)
            gv_ref[:, hs] = (r * yy).astype(bf16)
            ubs[h] = ub
            pm = jnp.where(bi <= bj, nt(ub, g), 0.0).astype(bf16)
            sm = (
                jnp.where(bi < bj, nt(ub, yb), 0.0) + jnp.where(bi > bj, nt(yb, ub), 0.0)
            ).astype(bf16)
            ka = -r * (mm(ub, l) + mm(yb, w) + mm(pm, q) - r * mm(sm, kb))
            k = kf[h]
            along = jnp.sum(k * ka, axis=1, keepdims=True)
            raws.append(((ka - k * along) * invf[h]).astype(bf16))
        g, a = spot(half, 0, 0)
        raw_all[half, g, a] = jnp.concatenate(raws, axis=1)
        ag_send(half, 0, 0, 0, 1)
        ag_send(half, 0, 0, 0, -1)

    raw = jnp.concatenate(
        [raw_all[half, spot(half, 0, 0)[0], spot(half, 0, 0)[1]] for half in range(2)], axis=1
    )

    def part(off):
        to = (zme + off) % NZ
        rows = pl.ds(pl.multiple_of(to * NH * W, NH * W), NH * W)
        out = nt(raw, kw_ref[rows, :])
        zs[off, 0] = out[:, :2 * W].astype(bf16)
        zs[off, 1] = out[:, 2 * W:].astype(bf16)

    def z_copy(way, n, half):
        off = 4 - n if way == 0 else (4 + n) % NZ
        return head_copy(
            zs.at[off, half], zr.at[way, n, half], z_ss, z_rs.at[way, 2 * n + half],
            up if way == 0 else down,
        )

    def z_add(way, n, half):
        off = 4 - n if way == 0 else (4 + n) % NZ
        z_copy(way, n - 1, half).wait_recv()
        zs[off, half] = (
            zs[off, half].astype(f32) + zr[way, n - 1, half].astype(f32)
        ).astype(bf16)
        z_copy(way, n, half).start()

    part(4)
    z_copy(0, 0, 0).start()
    z_copy(1, 0, 1).start()
    part(3)
    z_copy(0, 1, 1).start()
    part(5)
    z_copy(1, 1, 0).start()

    for half in range(2):
        second_leg(half, 0)
        first_leg_on(half)
        second_leg(half, -1)
        second_leg(half, 1)

    part(2)
    part(6)
    z_add(0, 1, 0)
    z_add(1, 1, 1)
    z_add(0, 2, 1)
    z_add(1, 2, 0)
    for half in range(2):
        ag_wait(half, 2, 0, 0, 2)
        ag_wait(half, 2, 0, 0, 3)
        second_leg(half, 2)
        sib_copy(half, 0, core).start()
    part(1)
    part(7)
    z_add(0, 2, 0)
    z_add(1, 2, 1)
    for half in range(2):
        second_leg_on(half, 0)
    z_add(0, 3, 1)
    z_add(1, 3, 0)
    part(0)
    for half in range(2):
        second_leg_on(half, -1)
    z_add(0, 3, 0)
    z_add(1, 3, 1)
    for half in range(2):
        second_leg_on(half, 1)
    for half in range(2):
        second_leg_on(half, 2)
        sib_copy(half, -1, core).start()
        sib_copy(half, 1, core).start()

    for dist in (2, 3):
        for way in (1, -1):
            tz_arrived(dist, way)
            tz(dist, way).start()
    for way in (1, -1):
        tz_arrived(4, way)

    def turn(b, c):
        for cc in range(NC):
            for a in range(4):
                t = tokcol[:, (cc * NY + b) * NX + a].reshape(W, W).T
                tok_t[0, cc, b, :, a * W:a * W + W] = t
                tok_t[1, cc, a, :, pl.ds(pl.multiple_of(b * W, W), W)] = t
        return c

    lax.fori_loop(0, 4, turn, 0)

    for h in range(NH):
        hs = slice(h * W, h * W + W)
        bi, bj = batch_of()
        g = g_ref[:, hs]
        low = jnp.where(bi >= bj, nt(g, ubs[h]), 0.0).astype(bf16)
        gq_ref[:, hs] = (mm(g, wl[2 * h]) - rates[h] * mm(low, kbs[h])).astype(bf16)

    for half in range(2):
        z_copy(0, 3, half).wait_recv()
        z_copy(1, 3, half).wait_recv()
        gt_ref[:, 2 * W * half:2 * W * (half + 1)] = (
            zs[0, half].astype(f32) + zr[0, 3, half].astype(f32) + zr[1, 3, half].astype(f32)
        ).astype(bf16)

    def product(half, db, cc):
        b = (mine[half][1] + db) % 4
        return mm(tok_t[half, cc, b], raw_all[half, cc * 4 + b].reshape(4 * W, 2 * W))

    accs = [
        product(half, 0, core) + product(half, -1, core) + product(half, 1, core)
        for half in range(2)
    ]
    for half in range(2):
        for da in (0, -1, 1, 2):
            ag_wait(half, da, 2, 1, 2)
            ag_wait(half, da, 2, 1, 3)
        sib_copy(half, 2, core).start()
        accs[half] = accs[half] + product(half, 2, core)
    for half in range(2):
        for db in (0, -1, 1, 2):
            sib_copy(half, db, 1 - core).wait_recv()
            accs[half] = accs[half] + product(half, db, 1 - core)
        gkw_ref[:, 2 * W * half:2 * W * (half + 1)] = accs[half]

    tok_sum.wait_send()
    head_copy(tokcol.at[pl.ds(0, 7)], tokcol.at[pl.ds(0, 7)], tz_ss, tz_rs.at[0], up).wait_send()
    ef_sum.wait_send()
    for to_pos in range(1, NY):
        @pl.when(to_pos > pos)
        def _():
            seq_copy(tot_send, tot_recv.at[0], tot_ss.at[to_pos], tot_rs.at[0], sib).wait_send()
    x_sum.wait_send()
    for half in range(2):
        ref = kw_ref.at[pl.ds(0, 31 * W // 2)]
        seq_copy(ref, ref, ag_ss.at[half], sib_rs.at[half, 0], sib).wait_send()
    some_z = zs.at[pl.ds(0, 7)]
    head_copy(some_z, some_z, z_ss, z_rs.at[0, 0], up).wait_send()


def hand_over(a0, a1, a2, a3, b0, b1, b2, b3):
    for a, b in ((a0, b0), (a1, b1), (a2, b2), (a3, b3)):
        b[...] = a[...]


def per_device(tokens, key_weight, queries, values, grad_out, inner_start, head_rate):
    vmem = pl.BlockSpec(memory_space=pltpu.VMEM)
    smem = pl.BlockSpec(memory_space=pltpu.SMEM)
    anywhere = pl.BlockSpec(memory_space=pl.ANY)
    cols = NH * W
    sem = pltpu.SemaphoreType.DMA
    shapes = (
        jax.ShapeDtypeStruct((W, cols), bf16),
        jax.ShapeDtypeStruct((W, cols), f32),
        jax.ShapeDtypeStruct((W, cols), bf16),
        jax.ShapeDtypeStruct((W, cols), bf16),
    )
    outs = pl.pallas_call(
        kernel,
        out_shape=shapes,
        in_specs=[anywhere] * 6 + [smem],
        out_specs=(vmem,) * 4,
        scratch_shapes=[
            pltpu.VMEM(tokens.shape, bf16),
            pltpu.VMEM(key_weight.shape, bf16),
            pltpu.VMEM((W, cols), bf16),
            pltpu.VMEM((W, cols), bf16),
            pltpu.VMEM((W, cols), bf16),
            pltpu.VMEM((NH, W, W), f32),
            pltpu.VMEM((NZ, NS, TZ, W), bf16),
            pltpu.VMEM((2, NC, 4, W, 4 * W), bf16),
            pltpu.VMEM((2, NH, 2 * W, W), bf16),
            pltpu.VMEM((ROW, 2 * W, W), bf16),
            pltpu.VMEM((2 * W, W), bf16),
            pltpu.VMEM((NY, 2 * W, W), bf16),
            pltpu.VMEM((6, 2 * W, W), f32),
            pltpu.VMEM((W, W), f32),
            pltpu.VMEM((ROW, W, W), bf16),
            pltpu.VMEM((2 * NH, W, W), bf16),
            pltpu.VMEM((NH, W, W), f32),
            pltpu.VMEM((NH, W, W), f32),
            pltpu.VMEM((NH, W, W), bf16),
            pltpu.VMEM((NH, W, W), bf16),
            pltpu.VMEM((NH, W, W), f32),
            pltpu.VMEM((NH, W, W), bf16),
            pltpu.VMEM((NH, W, W), f32),
            pltpu.VMEM((NH, W, W), bf16),
            pltpu.VMEM((2, NC * 4, 4, W, 2 * W), bf16),
            pltpu.VMEM((NZ, 2, W, 2 * W), bf16),
            pltpu.VMEM((2, 4, 2, W, 2 * W), bf16),
            sem((5 + KW_PARTS,)),
            sem, sem,
            sem, sem((NZ,)),
            sem, sem,
            sem((NY,)), sem((NY,)),
            sem, sem,
            sem((2,)), sem((2, 20)), sem((2, 4)),
            sem, sem((2, 8)),
        ],
        compiler_params=pltpu.CompilerParams(
            collective_id=0, has_side_effects=True, vmem_limit_bytes=56 * 1024 * 1024
        ),
        name="layer",
    )(tokens, key_weight, queries, values, grad_out, inner_start, head_rate)
    return pl.pallas_call(
        hand_over,
        out_shape=shapes,
        in_specs=[vmem] * 4,
        out_specs=(vmem,) * 4,
        name="hand_over",
    )(*outs)


def solution(mesh):
    placed = (
        P("seq", None),
        P(None, "head"),
        P("seq", "head"),
        P("seq", "head"),
        P("seq", "head"),
        P("head", None, None),
        P("head"),
    )
    return jax.shard_map(
        per_device,
        mesh=mesh,
        in_specs=placed,
        out_specs=(P("seq", "head"),) * 4,
        check_vma=False,
    )
```

```python
import jax
import jax.numpy as jnp
from jax import lax
from jax.experimental import pallas as pl
from jax.experimental.pallas import tpu as pltpu
from jax.sharding import PartitionSpec as P

MESH = pl.DeviceIdType.MESH
bf16 = jnp.bfloat16
f32 = jnp.float32
rate_base = 0.1
norm_eps = 1e-06
W = 128
NH = 4
NX, NY, NC = 4, 4, 2
ROW = NX * NC
NZ = 8
KW_PARTS = 4


def mm(a, b):
    return lax.dot_general(a, b, (((1,), (0,)), ((), ())), preferred_element_type=f32)


def nt(a, b):
    return lax.dot_general(a, b, (((1,), (1,)), ((), ())), preferred_element_type=f32)


def tn(a, b):
    return lax.dot_general(a, b, (((0,), (0,)), ((), ())), preferred_element_type=f32)


def batch_of():
    rows = lax.broadcasted_iota(jnp.int32, (W, W), 0) >> 4
    cols = lax.broadcasted_iota(jnp.int32, (W, W), 1) >> 4
    return rows, cols


def local_maps(kraw, v, q, g, r):
    bi, bj = batch_of()
    inv = lax.rsqrt(jnp.sum(kraw * kraw, axis=1, keepdims=True) + norm_eps)
    k = kraw * inv
    kb = k.astype(bf16)
    m = r * nt(kb, kb)
    x1 = jnp.where(((bi >> 1) == (bj >> 1)) & (bi > bj), m, 0.0)
    x2 = jnp.where(((bi >> 2) == (bj >> 2)) & ((bi >> 1) > (bj >> 1)), m, 0.0)
    x3 = jnp.where((bi >> 2) > (bj >> 2), m, 0.0)
    rows = lax.broadcasted_iota(jnp.int32, (W, W), 0)
    cols = lax.broadcasted_iota(jnp.int32, (W, W), 1)
    t1 = jnp.where(rows == cols, 1.0, 0.0) - x1
    t1b = t1.astype(bf16)
    t2 = t1 - mm(mm(t1b, x2.astype(bf16)).astype(bf16), t1b)
    t2b = t2.astype(bf16)
    t3 = t2 - mm(mm(t2b, x3.astype(bf16)).astype(bf16), t2b)
    tb = t3.astype(bf16)
    tk = mm(tb, kb).astype(bf16)
    tv = mm(tb, v)
    z = mm(jnp.where(bi <= bj, nt(kb, q), 0.0).astype(bf16), g).astype(bf16)
    ttk = tn(tb, kb).astype(bf16)
    ttz = tn(tb, z)
    e0 = (-r * tn(tk, kb)).astype(bf16)
    f0 = (r * tn(tv.astype(bf16), kb)).astype(bf16)
    e1 = (-r * tn(kb, tk)).astype(bf16)
    f1 = (tn(g, q) - r * tn(ttz.astype(bf16), kb)).astype(bf16)
    return k, inv, kb, tk, tv, ttk, ttz, e0, f0, e1, f1


def join(a, b):
    return a.astype(f32) + b.astype(f32) + mm(a.astype(bf16), b[:W].astype(bf16))


def apply(state, m):
    return state + mm(state.astype(bf16), m[:W].astype(bf16)) + m[W:].astype(f32)


def kernel(
    tok_hbm, kw_hbm, q_hbm, v_hbm, g_hbm, w0_hbm, rate_ref,
    gt_ref, gkw_ref, gq_ref, gv_ref,
    tok_ref, kw_ref, q_ref, v_ref, g_ref, w0_ref, kraw_ref,
    tokcol, tok_t, maps, sib_maps, first, chip_maps, ef_recv, tot_send, tot_recv, nodes,
    state, x_send, x_in, x_sib, wl,
    kf, invf, kbs, tks, tvs, ttks, ttzs, ubs, raw_all, psum, rs_s, rs_r, zs, zr,
    in_s, tok_ss, tok_rs, tz_ss, tz_rs, sm_ss, sm_rs, ef_ss, ef_rs, tot_ss, tot_rs,
    x_ss, x_rs, xs_ss, xs_rs, ag_ss, ag_rs, sib_rs, rs_ss, rs_rs, z_ss, z_rs,
):
    me = lax.axis_index("seq")
    zme = lax.axis_index("head")
    y = me // ROW
    p = me % ROW
    x = p // NC
    core = p % NC
    sib = me + 1 - 2 * core
    hands = x // 2 == core

    def dev(yy, xx, cc):
        return (yy * NX + xx) * NC + cc

    def seq_copy(src, dst, ss, rs, to):
        return pltpu.make_async_remote_copy(
            src_ref=src, dst_ref=dst, send_sem=ss, recv_sem=rs,
            device_id={"seq": to}, device_id_type=MESH,
        )

    def head_copy(src, dst, ss, rs, to):
        return pltpu.make_async_remote_copy(
            src_ref=src, dst_ref=dst, send_sem=ss, recv_sem=rs,
            device_id={"head": to}, device_id_type=MESH,
        )

    deep = kw_ref.shape[0] // KW_PARTS
    loads = [pltpu.make_async_copy(tok_hbm, tok_ref, in_s.at[0])]
    for i in range(KW_PARTS):
        rows = pl.ds(i * deep, deep)
        loads.append(pltpu.make_async_copy(kw_hbm.at[rows], kw_ref.at[rows], in_s.at[1 + i]))
    for i, (src, dst) in enumerate(
        ((q_hbm, q_ref), (v_hbm, v_ref), (g_hbm, g_ref), (w0_hbm, w0_ref))
    ):
        loads.append(pltpu.make_async_copy(src, dst, in_s.at[1 + KW_PARTS + i]))
    for load in loads:
        load.start()

    barrier = pltpu.get_barrier_semaphore()

    def greet_seq(to):
        pl.semaphore_signal(barrier, inc=1, device_id={"seq": to}, device_id_type=MESH)

    for i in range(1, ROW):
        greet_seq(y * ROW + (p + i) % ROW)
    for i in range(1, NY):
        for cc in range(NC):
            greet_seq(dev((y + i) % NY, x, cc))
    z_at = [(zme + i) % NZ for i in range(NZ)]
    for i in (1, 2, 6, 7):
        pl.semaphore_signal(
            barrier, inc=1, device_id={"head": z_at[i]}, device_id_type=MESH
        )
    partners = ROW - 1 + NC * (NY - 1) + 4

    loads[0].wait()
    kraw = None
    for i in range(KW_PARTS):
        loads[1 + i].wait()
        rows = slice(i * deep, (i + 1) * deep)
        prod = mm(tok_ref[:, rows], kw_ref[rows, :])
        kraw = prod if kraw is None else kraw + prod
    kraw_ref[...] = kraw
    for load in loads[1 + KW_PARTS:]:
        load.wait()
    for i in range(NH):
        h = (2 * (1 - core) + i) % NH
        hs = pl.ds(pl.multiple_of(h * W, W), W)
        k, inv, kb, tk, tv, ttk, ttz, e0, f0, e1, f1 = local_maps(
            kraw_ref[:, hs], v_ref[:, hs], q_ref[:, hs], g_ref[:, hs], rate_base * rate_ref[h]
        )
        kf[h] = k
        invf[h] = jnp.broadcast_to(inv, (W, W))
        kbs[h] = kb
        tks[h] = tk
        tvs[h] = tv
        ttks[h] = ttk
        ttzs[h] = ttz
        maps[h, 0, :W] = e0
        maps[h, 0, W:] = f0
        maps[h, 1, :W] = e1
        maps[h, 1, W:] = f1
        if i == 0:
            pl.semaphore_wait(barrier, partners)
        if i < 2:
            seq_copy(maps.at[h], sib_maps.at[i], sm_ss, sm_rs, sib).start()

    sm_sum = seq_copy(sib_maps, sib_maps, sm_ss, sm_rs, sib)
    sm_sum.wait_recv()
    for i in range(2):
        h = 2 * core + i
        for role in range(2):
            here, there = maps[h, role], sib_maps[i, role]
            mine_first = core == role
            one = jnp.where(mine_first, here, there)
            first[i, role] = one
            chip_maps[i, role] = join(one, jnp.where(mine_first, there, here)).astype(bf16)
            slot = x if role == 0 else NX - 1 - x
            local = (x == h) & (core == role)

            @pl.when(jnp.logical_not(local))
            def _():
                seq_copy(
                    chip_maps.at[i, role], ef_recv.at[slot], ef_ss, ef_rs, dev(y, h, role)
                ).start()

            @pl.when(local)
            def _():
                ef_recv[slot] = chip_maps[i, role]

    zp = zme % 2
    half_rows = pl.ds(pl.multiple_of(zp * (W // 2), W // 2), W // 2)
    src_me = y * NC + core

    def tok_cols(yy, xx, cc):
        return pl.ds(pl.multiple_of(dev(yy, xx, cc) * W, W), W)

    def tok_start(yy, cc):
        for xx in range(NX):
            seq_copy(
                tok_ref.at[half_rows, tok_cols(yy, xx, cc)], tokcol.at[zp, src_me, xx],
                tok_ss, tok_rs, dev(yy, x, cc),
            ).start()

    for i in (2, 1, 3):
        for cc in range(NC):
            tok_start((y + i) % NY, cc)
    tok_start(y, 1 - core)
    for xx in range(NX):
        tokcol[zp, src_me, xx] = tok_ref[half_rows, tok_cols(y, xx, core)]
    tok_all = tokcol.at[0, pl.ds(0, 2 * NY - 1)]
    tok_sum = seq_copy(tok_all, tok_all, tok_ss, tok_rs, sib)
    tz_out = head_copy(tokcol.at[zp], tokcol.at[zp], tz_ss, tz_rs, zme + 1 - 2 * zp)
    tz_in = head_copy(tokcol.at[1 - zp], tokcol.at[1 - zp], tz_ss, tz_rs, zme + 1 - 2 * zp)

    def count(ref, ss, rs, act):
        few = ref.at[pl.ds(0, NX - 1)]

        @pl.when(hands)
        def _():
            act(seq_copy(few, few, ss, rs, sib))

        @pl.when(jnp.logical_not(hands))
        def _():
            act(seq_copy(ref, ref, ss, rs, sib))

    count(ef_recv, ef_ss, ef_rs, lambda c: c.wait_recv())
    for i in range(2):
        nodes[i] = join(ef_recv[2 * i], ef_recv[2 * i + 1])
    tot_send[...] = join(nodes[0], nodes[1]).astype(bf16)

    pos = jnp.where(core == 0, y, NY - 1 - y)
    for to_pos in range(NY - 1, 0, -1):
        to_y = jnp.where(core == 0, to_pos, NY - 1 - to_pos)

        @pl.when(to_pos > pos)
        def _():
            seq_copy(
                tot_send, tot_recv.at[pos], tot_ss.at[to_pos], tot_rs.at[pos],
                dev(to_y, x, core),
            ).start()

    tok_sum.wait_recv()
    tz_out.start()

    state[...] = jnp.where(core == 0, w0_ref[x].T, 0.0)
    for j in range(NY - 1):
        frm_y = jnp.where(core == 0, j, NY - 1 - j)

        @pl.when(j < pos)
        def _():
            seq_copy(
                tot_send, tot_recv.at[j], tot_ss.at[0], tot_rs.at[j], dev(frm_y, x, core)
            ).wait_recv()
            state[...] = apply(state[...], tot_recv[j])

    xs = [None] * NX
    xs[0] = state[...]
    xs[2] = apply(xs[0], nodes[0])
    xs[1] = apply(xs[0], ef_recv[0])
    xs[3] = apply(xs[2], ef_recv[2])
    spot = 2 * (x % 2) + core
    for slot in range(NX):
        x_send[slot] = xs[slot].astype(bf16)
        to = jnp.where(core == 0, slot, NX - 1 - slot)
        local = hands & (to == x)

        @pl.when(jnp.logical_not(local))
        def _():
            seq_copy(x_send.at[slot], x_in.at[spot], x_ss, x_rs, dev(y, to, x // 2)).start()

        @pl.when(local)
        def _():
            x_in[spot] = x_send[slot]

    count(x_in, x_ss, x_rs, lambda c: c.wait_recv())
    for i in range(2):
        for role in range(2):
            at_first = x_in[2 * i + role]
            at_second = apply(at_first.astype(f32), first[i, role]).astype(bf16)
            wl[2 * core + i, role] = jnp.where(core == role, at_first, at_second)
            x_sib[i, role] = jnp.where(core == role, at_second, at_first)
    own_two = wl.at[pl.ds(2 * core, 2)]
    other_two = wl.at[pl.ds(2 * (1 - core), 2)]
    x_out = seq_copy(x_sib, own_two, xs_ss, xs_rs, sib)
    x_out.start()

    below, above = dev((y + NY - 1) % NY, x, core), dev((y + 1) % NY, x, core)
    src_at = [((y + i) % NY) * NC + core for i in range(NY)]
    low, high = pl.ds(0, W // 2), pl.ds(W // 2, W // 2)

    def ag_copy(half, off, kind, to):
        ref = raw_all.at[half, src_at[off]]
        if kind >= 2:
            ref = raw_all.at[half, src_at[off], low if kind == 2 else high]
        return seq_copy(ref, ref, ag_ss.at[half], ag_rs.at[half, kind], to)

    def sib_copy(half, off, cc):
        ref = raw_all.at[half, ((y + off) % NY) * NC + cc]
        return seq_copy(ref, ref, ag_ss.at[half], sib_rs.at[half, off], sib)

    rates = [rate_base * rate_ref[h] for h in range(NH)]
    raws = []
    for half in range(2):
        @pl.when(core != half)
        def _():
            seq_copy(other_two, other_two, xs_ss, xs_rs, sib).wait_recv()

        for h in (2 * half, 2 * half + 1):
            hs = slice(h * W, h * W + W)
            bi, bj = batch_of()
            r = rates[h]
            w, l = wl[h, 0], wl[h, 1]
            q, g, kb = q_ref[:, hs], g_ref[:, hs], kbs[h]
            ub = (nt(tks[h], w) - tvs[h]).astype(bf16)
            yy = nt(ttks[h], l) + ttzs[h]
            yb = yy.astype(bf16)
            gv_ref[:, hs] = (r * yy).astype(bf16)
            ubs[h] = ub
            pm = jnp.where(bi <= bj, nt(ub, g), 0.0).astype(bf16)
            sm = (
                jnp.where(bi < bj, nt(ub, yb), 0.0) + jnp.where(bi > bj, nt(yb, ub), 0.0)
            ).astype(bf16)
            ka = -r * (mm(ub, l) + mm(yb, w) + mm(pm, q) - r * mm(sm, kb))
            k = kf[h]
            along = jnp.sum(k * ka, axis=1, keepdims=True)
            raws.append(((ka - k * along) * invf[h]).astype(bf16))
        raw_all[half, src_me] = jnp.concatenate(raws[-2:], axis=1)
        ag_copy(half, 0, 0, above).start()
        ag_copy(half, 0, 1, below).start()
        sib_copy(half, 0, core).start()

    raw = jnp.concatenate([raw_all[0, src_me], raw_all[1, src_me]], axis=1)

    def part(off):
        rows = pl.ds(pl.multiple_of(z_at[off] * NH * W, NH * W), NH * W)
        out = nt(raw, kw_ref[rows, :])
        zs[off, 0] = out[:, :2 * W].astype(bf16)
        zs[off, 1] = out[:, 2 * W:].astype(bf16)

    def z_copy(way, n, half):
        off = 4 - n if way == 0 else (4 + n) % NZ
        to = (2 if n == 0 else 1) if way == 0 else (6 if n == 0 else 7)
        return head_copy(
            zs.at[off, half], zr.at[way, n, half], z_ss, z_rs.at[way, 2 * n + half], z_at[to]
        )

    def z_add(way, n, half):
        off = 4 - n if way == 0 else (4 + n) % NZ
        z_copy(way, n - 1, half).wait_recv()
        total = zs[off, half].astype(f32) + zr[way, n - 1, half].astype(f32)
        if n == 2 and half == way:
            z_copy(way, 0, half).wait_recv()
            total = total + zr[way, 0, half].astype(f32)
        zs[off, half] = total.astype(bf16)
        z_copy(way, n, half).start()

    part(3)
    z_copy(0, 1, 1).start()
    z_copy(0, 1, 0).start()
    part(5)
    z_copy(1, 1, 0).start()
    z_copy(1, 1, 1).start()
    part(4)
    z_copy(0, 0, 0).start()
    z_copy(1, 0, 1).start()
    part(2)
    part(6)

    def relay(half):
        ag_copy(half, 3, 0, sib).wait_recv()
        ag_copy(half, 3, 2, above).start()
        sib_copy(half, 3, core).start()
        ag_copy(half, 1, 1, sib).wait_recv()
        ag_copy(half, 1, 3, below).start()
        sib_copy(half, 1, core).start()

    def far(half):
        ag_copy(half, 2, 2, sib).wait_recv()
        ag_copy(half, 2, 3, sib).wait_recv()
        sib_copy(half, 2, core).start()

    relay(0)
    relay(1)
    z_add(0, 2, 1)
    z_add(1, 2, 0)
    z_add(0, 2, 0)
    z_add(1, 2, 1)

    tz_in.wait_recv()

    def turn(src, c):
        cols = pl.ds(pl.multiple_of(src * W, W), W)
        for xx in range(NX):
            both = jnp.concatenate([tokcol[0, src, xx], tokcol[1, src, xx]], axis=0)
            tok_t[xx * W:xx * W + W, cols] = both.T
        return c

    lax.fori_loop(0, NC * NY, turn, 0)
    part(1)
    part(7)
    far(0)
    z_add(0, 3, 1)
    z_add(1, 3, 0)

    x_at = [(x + i) % NX for i in range(NX)]
    right, left = dev(y, x_at[1], core), dev(y, x_at[3], core)

    def rs_copy(half, off, piece):
        rows = low if piece == 0 else high
        to_right = off == 1 or (off == 2 and piece == 0)
        return seq_copy(
            rs_s.at[half, off, rows], rs_r.at[half, off, rows], rs_ss.at[half],
            rs_rs.at[half, 2 * off + piece], right if to_right else left,
        )

    def products(half):
        for off in range(NY):
            sib_copy(half, off, 1 - core).wait_recv()
        out = mm(tok_t[...], raw_all[half].reshape(NC * NY * W, 2 * W))
        for xx in range(NX):
            psum[half, xx] = out[xx * W:xx * W + W]
        for off in (2, 1, 3):
            rs_s[half, off] = psum[half, x_at[off]].astype(bf16)
            if off == 2:
                rs_copy(half, 2, 0).start()
                rs_copy(half, 2, 1).start()
            else:
                rs_copy(half, off, 1 if off == 1 else 0).start()

    def rs_add(half):
        for off, piece in ((1, 0), (3, 1)):
            rows = slice(0, W // 2) if piece == 0 else slice(W // 2, W)
            rs_copy(half, 2, piece).wait_recv()
            rs_s[half, off, rows] = (
                psum[half, x_at[off], rows] + rs_r[half, 2, rows].astype(f32)
            ).astype(bf16)
            rs_copy(half, off, piece).start()

    def rs_end(half):
        for off in (1, 3):
            for piece in range(2):
                rs_copy(half, off, piece).wait_recv()
        gkw_ref[:, 2 * W * half:2 * W * (half + 1)] = (
            psum[half, x] + rs_r[half, 1].astype(f32) + rs_r[half, 3].astype(f32)
        )

    products(0)
    z_add(0, 3, 0)
    z_add(1, 3, 1)
    far(1)
    products(1)
    part(0)

    def grad_query(h):
        hs = slice(h * W, h * W + W)
        bi, bj = batch_of()
        g = g_ref[:, hs]
        lower = jnp.where(bi >= bj, nt(g, ubs[h]), 0.0).astype(bf16)
        gq_ref[:, hs] = (mm(g, wl[h, 0]) - rates[h] * mm(lower, kbs[h])).astype(bf16)

    grad_query(0)
    grad_query(1)
    rs_add(0)
    grad_query(2)
    grad_query(3)
    rs_add(1)

    for half in range(2):
        z_copy(0, 3, half).wait_recv()
        z_copy(1, 3, half).wait_recv()
        gt_ref[:, 2 * W * half:2 * W * (half + 1)] = (
            zs[0, half].astype(f32) + zr[0, 3, half].astype(f32) + zr[1, 3, half].astype(f32)
        ).astype(bf16)
    rs_end(0)
    rs_end(1)

    sm_sum.wait_send()
    count(ef_recv, ef_ss, ef_rs, lambda c: c.wait_send())
    tok_sum.wait_send()
    tz_out.wait_send()
    for to_pos in range(1, NY):
        @pl.when(to_pos > pos)
        def _():
            seq_copy(tot_send, tot_recv.at[0], tot_ss.at[to_pos], tot_rs.at[0], sib).wait_send()
    count(x_in, x_ss, x_rs, lambda c: c.wait_send())
    x_out.wait_send()
    for half in range(2):
        ref = raw_all.at[half, pl.ds(0, 7)]
        seq_copy(ref, ref, ag_ss.at[half], sib_rs.at[half, 0], sib).wait_send()
        ref = rs_s.at[half, pl.ds(0, 3)]
        seq_copy(ref, ref, rs_ss.at[half], rs_rs.at[half, 0], sib).wait_send()
    some_z = zs.at[pl.ds(0, 7)]
    head_copy(some_z, some_z, z_ss, z_rs.at[0, 0], z_at[1]).wait_send()


def hand_over(a0, a1, a2, a3, b0, b1, b2, b3):
    for a, b in ((a0, b0), (a1, b1), (a2, b2), (a3, b3)):
        b[...] = a[...]


def per_device(tokens, key_weight, queries, values, grad_out, inner_start, head_rate):
    vmem = pl.BlockSpec(memory_space=pltpu.VMEM)
    smem = pl.BlockSpec(memory_space=pltpu.SMEM)
    anywhere = pl.BlockSpec(memory_space=pl.ANY)
    cols = NH * W
    sem = pltpu.SemaphoreType.DMA
    shapes = (
        jax.ShapeDtypeStruct((W, cols), bf16),
        jax.ShapeDtypeStruct((W, cols), f32),
        jax.ShapeDtypeStruct((W, cols), bf16),
        jax.ShapeDtypeStruct((W, cols), bf16),
    )
    outs = pl.pallas_call(
        kernel,
        out_shape=shapes,
        in_specs=[anywhere] * 6 + [smem],
        out_specs=(vmem,) * 4,
        scratch_shapes=[
            pltpu.VMEM(tokens.shape, bf16),
            pltpu.VMEM(key_weight.shape, bf16),
            pltpu.VMEM((W, cols), bf16),
            pltpu.VMEM((W, cols), bf16),
            pltpu.VMEM((W, cols), bf16),
            pltpu.VMEM((NH, W, W), f32),
            pltpu.VMEM((W, cols), f32),
            pltpu.VMEM((2, NC * NY, NX, W // 2, W), bf16),
            pltpu.VMEM((NX * W, NC * NY * W), bf16),
            pltpu.VMEM((NH, 2, 2 * W, W), bf16),
            pltpu.VMEM((2, 2, 2 * W, W), bf16),
            pltpu.VMEM((2, 2, 2 * W, W), bf16),
            pltpu.VMEM((2, 2, 2 * W, W), bf16),
            pltpu.VMEM((NX, 2 * W, W), bf16),
            pltpu.VMEM((2 * W, W), bf16),
            pltpu.VMEM((NY, 2 * W, W), bf16),
            pltpu.VMEM((2, 2 * W, W), f32),
            pltpu.VMEM((W, W), f32),
            pltpu.VMEM((NX, W, W), bf16),
            pltpu.VMEM((4, W, W), bf16),
            pltpu.VMEM((2, 2, W, W), bf16),
            pltpu.VMEM((NH, 2, W, W), bf16),
            pltpu.VMEM((NH, W, W), f32),
            pltpu.VMEM((NH, W, W), f32),
            pltpu.VMEM((NH, W, W), bf16),
            pltpu.VMEM((NH, W, W), bf16),
            pltpu.VMEM((NH, W, W), f32),
            pltpu.VMEM((NH, W, W), bf16),
            pltpu.VMEM((NH, W, W), f32),
            pltpu.VMEM((NH, W, W), bf16),
            pltpu.VMEM((2, NC * NY, W, 2 * W), bf16),
            pltpu.VMEM((2, NX, W, 2 * W), f32),
            pltpu.VMEM((2, NX, W, 2 * W), bf16),
            pltpu.VMEM((2, NX, W, 2 * W), bf16),
            pltpu.VMEM((NZ, 2, W, 2 * W), bf16),
            pltpu.VMEM((2, 4, 2, W, 2 * W), bf16),
            sem((5 + KW_PARTS,)),
            sem, sem, sem, sem,
            sem, sem, sem, sem,
            sem((NY,)), sem((NY,)),
            sem, sem, sem, sem,
            sem((2,)), sem((2, 4)), sem((2, 4)),
            sem((2,)), sem((2, 8)),
            sem, sem((2, 8)),
        ],
        compiler_params=pltpu.CompilerParams(
            collective_id=0, has_side_effects=True, vmem_limit_bytes=56 * 1024 * 1024
        ),
        name="layer",
    )(tokens, key_weight, queries, values, grad_out, inner_start, head_rate)
    return pl.pallas_call(
        hand_over,
        out_shape=shapes,
        in_specs=[vmem] * 4,
        out_specs=(vmem,) * 4,
        name="hand_over",
    )(*outs)


def solution(mesh):
    placed = (
        P("seq", None),
        P(None, "head"),
        P("seq", "head"),
        P("seq", "head"),
        P("seq", "head"),
        P("head", None, None),
        P("head"),
    )
    return jax.shard_map(
        per_device,
        mesh=mesh,
        in_specs=placed,
        out_specs=(P("seq", "head"),) * 4,
        check_vma=False,
    )
```

```python
import jax
import jax.numpy as jnp
from jax import lax
from jax.experimental import pallas as pl
from jax.experimental.pallas import tpu as pltpu
from jax.sharding import PartitionSpec as P

MESH = pl.DeviceIdType.MESH
bf16 = jnp.bfloat16
f32 = jnp.float32
rate_base = 0.1
norm_eps = 1e-06
W = 128
NH = 4
NX, NY, NC = 4, 4, 2
ROW = NX * NC
NZ = 8
KW_PARTS = 4


def mm(a, b):
    return lax.dot_general(a, b, (((1,), (0,)), ((), ())), preferred_element_type=f32)


def nt(a, b):
    return lax.dot_general(a, b, (((1,), (1,)), ((), ())), preferred_element_type=f32)


def tn(a, b):
    return lax.dot_general(a, b, (((0,), (0,)), ((), ())), preferred_element_type=f32)


def batch_of():
    rows = lax.broadcasted_iota(jnp.int32, (W, W), 0) >> 4
    cols = lax.broadcasted_iota(jnp.int32, (W, W), 1) >> 4
    return rows, cols


def local_maps(kraws, vs, qs, gs, rs):
    n = range(len(rs))
    bi, bj = batch_of()
    rows = lax.broadcasted_iota(jnp.int32, (W, W), 0)
    cols = lax.broadcasted_iota(jnp.int32, (W, W), 1)
    eye = jnp.where(rows == cols, 1.0, 0.0)
    near = ((bi >> 1) == (bj >> 1)) & (bi > bj)
    middle = ((bi >> 2) == (bj >> 2)) & ((bi >> 1) > (bj >> 1))
    distant = (bi >> 2) > (bj >> 2)
    invs = [lax.rsqrt(jnp.sum(kr * kr, axis=1, keepdims=True) + norm_eps) for kr in kraws]
    ks = [kraws[i] * invs[i] for i in n]
    kbs = [k.astype(bf16) for k in ks]
    ms = [rs[i] * nt(kbs[i], kbs[i]) for i in n]
    zs = [jnp.where(bi <= bj, nt(kbs[i], qs[i]), 0.0).astype(bf16) for i in n]
    ts = [eye - jnp.where(near, m, 0.0) for m in ms]
    for mask in (middle, distant):
        tbs = [t.astype(bf16) for t in ts]
        us = [mm(tbs[i], jnp.where(mask, ms[i], 0.0).astype(bf16)).astype(bf16) for i in n]
        ts = [ts[i] - mm(us[i], tbs[i]) for i in n]
    zs = [mm(zs[i], gs[i]).astype(bf16) for i in n]
    qgs = [tn(gs[i], qs[i]) for i in n]
    tbs = [t.astype(bf16) for t in ts]
    tks = [mm(tbs[i], kbs[i]).astype(bf16) for i in n]
    tvs = [mm(tbs[i], vs[i]) for i in n]
    ttzs = [tn(tbs[i], zs[i]) for i in n]
    ttks = [tn(tbs[i], kbs[i]).astype(bf16) for i in n]
    e0s = [(-rs[i] * tn(tks[i], kbs[i])).astype(bf16) for i in n]
    e1s = [(-rs[i] * tn(kbs[i], tks[i])).astype(bf16) for i in n]
    f0s = [(rs[i] * tn(tvs[i].astype(bf16), kbs[i])).astype(bf16) for i in n]
    f1s = [(qgs[i] - rs[i] * tn(ttzs[i].astype(bf16), kbs[i])).astype(bf16) for i in n]
    return ks, invs, kbs, tks, tvs, ttks, ttzs, e0s, f0s, e1s, f1s


def final_rows(k, inv, kb, tk, tv, ttk, ttz, v, q, g, r, w, l):
    n = range(len(r))
    bi, bj = batch_of()
    ubs = [(nt(tk[i], w[i]) - tv[i]).astype(bf16) for i in n]
    ys = [nt(ttk[i], l[i]) + ttz[i] for i in n]
    ybs = [y.astype(bf16) for y in ys]
    pms = [jnp.where(bi <= bj, nt(ubs[i], g[i]), 0.0).astype(bf16) for i in n]
    sms = [
        jnp.where(
            bi < bj, nt(ubs[i], ybs[i]), jnp.where(bi > bj, nt(ybs[i], ubs[i]), 0.0)
        ).astype(bf16)
        for i in n
    ]
    kas = [mm(ubs[i], l[i]) + mm(ybs[i], w[i]) for i in n]
    kas = [kas[i] + mm(pms[i], q[i]) for i in n]
    kas = [-r[i] * (kas[i] - r[i] * mm(sms[i], kb[i])) for i in n]
    alongs = [jnp.sum(k[i] * kas[i], axis=1, keepdims=True) for i in n]
    raws = [((kas[i] - k[i] * alongs[i]) * inv[i]).astype(bf16) for i in n]
    return ubs, [(r[i] * ys[i]).astype(bf16) for i in n], raws


def join(a, b):
    return a.astype(f32) + b.astype(f32) + mm(a.astype(bf16), b[:W].astype(bf16))


def apply(state, m):
    return state + mm(state.astype(bf16), m[:W].astype(bf16)) + m[W:].astype(f32)


def kernel(
    tok_hbm, kw_hbm, q_hbm, v_hbm, g_hbm, w0_hbm, rate_ref,
    gt_ref, gkw_ref, gq_ref, gv_ref,
    tok_ref, kw_ref, q_ref, v_ref, g_ref, w0_ref, kraw_ref,
    tokcol, tok_t, maps, sib_maps, first, chip_maps, ef_recv, tot_send, tot_recv, nodes,
    state, x_send, x_in, x_sib, wl,
    kf, invf, kbs, tks, tvs, ttks, ttzs, ubs, raw_all, psum, rs_s, rs_r, zs, zr,
    in_s, tok_ss, tok_rs, tz_ss, tz_rs, sm_ss, sm_rs, ef_ss, ef_rs, tot_ss, tot_rs,
    x_ss, x_rs, xs_ss, xs_rs, ag_ss, ag_rs, sib_rs, rs_ss, rs_rs, z_ss, z_rs,
):
    me = lax.axis_index("seq")
    zme = lax.axis_index("head")
    y = me // ROW
    p = me % ROW
    x = p // NC
    core = p % NC
    sib = me + 1 - 2 * core
    hands = x // 2 == core

    def dev(yy, xx, cc):
        return (yy * NX + xx) * NC + cc

    def seq_copy(src, dst, ss, rs, to):
        return pltpu.make_async_remote_copy(
            src_ref=src, dst_ref=dst, send_sem=ss, recv_sem=rs,
            device_id={"seq": to}, device_id_type=MESH,
        )

    def head_copy(src, dst, ss, rs, to):
        return pltpu.make_async_remote_copy(
            src_ref=src, dst_ref=dst, send_sem=ss, recv_sem=rs,
            device_id={"head": to}, device_id_type=MESH,
        )

    deep = kw_ref.shape[0] // KW_PARTS
    loads = [pltpu.make_async_copy(tok_hbm, tok_ref, in_s.at[0])]
    for i in range(KW_PARTS):
        rows = pl.ds(i * deep, deep)
        loads.append(pltpu.make_async_copy(kw_hbm.at[rows], kw_ref.at[rows], in_s.at[1 + i]))
    for i, (src, dst) in enumerate(
        ((q_hbm, q_ref), (v_hbm, v_ref), (g_hbm, g_ref), (w0_hbm, w0_ref))
    ):
        loads.append(pltpu.make_async_copy(src, dst, in_s.at[1 + KW_PARTS + i]))
    for load in loads:
        load.start()

    barrier = pltpu.get_barrier_semaphore()

    def greet_seq(to):
        pl.semaphore_signal(barrier, inc=1, device_id={"seq": to}, device_id_type=MESH)

    for i in range(1, ROW):
        greet_seq(y * ROW + (p + i) % ROW)
    for i in range(1, NY):
        for cc in range(NC):
            greet_seq(dev((y + i) % NY, x, cc))
    z_at = [(zme + i) % NZ for i in range(NZ)]
    for i in (1, 2, 6, 7):
        pl.semaphore_signal(
            barrier, inc=1, device_id={"head": z_at[i]}, device_id_type=MESH
        )
    partners = ROW - 1 + NC * (NY - 1) + 4

    loads[0].wait()
    kraw = None
    for i in range(KW_PARTS):
        loads[1 + i].wait()
        rows = slice(i * deep, (i + 1) * deep)
        prod = mm(tok_ref[:, rows], kw_ref[rows, :])
        kraw = prod if kraw is None else kraw + prod
    kraw_ref[...] = kraw
    for load in loads[1 + KW_PARTS:]:
        load.wait()
    zp = zme % 2
    half_rows = pl.ds(pl.multiple_of(zp * (W // 2), W // 2), W // 2)
    src_me = y * NC + core

    def tok_cols(yy, xx, cc):
        return pl.ds(pl.multiple_of(dev(yy, xx, cc) * W, W), W)

    def tok_start(yy, cc):
        for xx in range(NX):
            seq_copy(
                tok_ref.at[half_rows, tok_cols(yy, xx, cc)], tokcol.at[zp, src_me, xx],
                tok_ss, tok_rs, dev(yy, x, cc),
            ).start()

    sm_out = seq_copy(maps.at[pl.ds(2 * (1 - core), 2)], sib_maps, sm_ss, sm_rs, sib)
    pl.semaphore_wait(barrier, partners)
    for cc in range(NC):
        tok_start((y + 2) % NY, cc)
    tok_start((y + 1) % NY, core)
    tok_start((y + 1) % NY, 1 - core)
    for cc in range(NC):
        tok_start((y + 3) % NY, cc)
    tok_start(y, 1 - core)
    for pair in range(2):
        base = 2 * ((1 - core + pair) % 2)
        cut = pl.ds(pl.multiple_of(base * W, 2 * W), 2 * W)

        def two(ref):
            both = ref[:, cut]
            return [both[:, :W], both[:, W:]]

        found = local_maps(
            two(kraw_ref), two(v_ref), two(q_ref), two(g_ref),
            [rate_base * rate_ref[base + i] for i in range(2)],
        )
        for i in range(2):
            h = base + i
            k, inv, kb, tk, tv, ttk, ttz, e0, f0, e1, f1 = [each[i] for each in found]
            maps[h, 0, :W] = e0
            maps[h, 0, W:] = f0
            maps[h, 1, :W] = e1
            maps[h, 1, W:] = f1
            kf[h] = k
            invf[h] = jnp.broadcast_to(inv, (W, W))
            kbs[h] = kb
            tks[h] = tk
            tvs[h] = tv
            ttks[h] = ttk
            ttzs[h] = ttz
        if pair == 0:
            sm_out.start()

    sm_sum = seq_copy(sib_maps, sib_maps, sm_ss, sm_rs, sib)
    sm_sum.wait_recv()
    i_far = jnp.where(hands, 1 - x % 2, x % 2)
    for step in range(2):
        i = i_far if step == 0 else 1 - i_far
        h = 2 * core + i
        for role in range(2):
            here, there = maps[h, role], sib_maps[i, role]
            mine_first = core == role
            one = jnp.where(mine_first, here, there)
            first[i, role] = one
            chip_maps[i, role] = join(one, jnp.where(mine_first, there, here)).astype(bf16)
            slot = x if role == 0 else NX - 1 - x
            local = (x == h) & (core == role)

            @pl.when(jnp.logical_not(local))
            def _():
                seq_copy(
                    chip_maps.at[i, role], ef_recv.at[slot], ef_ss, ef_rs, dev(y, h, role)
                ).start()

            @pl.when(local)
            def _():
                ef_recv[slot] = chip_maps[i, role]

    for xx in range(NX):
        tokcol[zp, src_me, xx] = tok_ref[half_rows, tok_cols(y, xx, core)]
    tok_all = tokcol.at[0, pl.ds(0, 2 * NY - 1)]
    tok_sum = seq_copy(tok_all, tok_all, tok_ss, tok_rs, sib)
    tz_out = head_copy(tokcol.at[zp], tokcol.at[zp], tz_ss, tz_rs, zme + 1 - 2 * zp)
    tz_in = head_copy(tokcol.at[1 - zp], tokcol.at[1 - zp], tz_ss, tz_rs, zme + 1 - 2 * zp)

    def count(ref, ss, rs, act):
        few = ref.at[pl.ds(0, NX - 1)]

        @pl.when(hands)
        def _():
            act(seq_copy(few, few, ss, rs, sib))

        @pl.when(jnp.logical_not(hands))
        def _():
            act(seq_copy(ref, ref, ss, rs, sib))

    count(ef_recv, ef_ss, ef_rs, lambda c: c.wait_recv())
    for i in range(2):
        nodes[i] = join(ef_recv[2 * i], ef_recv[2 * i + 1])
    tot_send[...] = join(nodes[0], nodes[1]).astype(bf16)

    pos = jnp.where(core == 0, y, NY - 1 - y)
    for to_pos in range(NY - 1, 0, -1):
        to_y = jnp.where(core == 0, to_pos, NY - 1 - to_pos)

        @pl.when(to_pos > pos)
        def _():
            seq_copy(
                tot_send, tot_recv.at[pos], tot_ss.at[to_pos], tot_rs.at[pos],
                dev(to_y, x, core),
            ).start()

    tok_sum.wait_recv()
    tz_out.start()

    state[...] = jnp.where(core == 0, w0_ref[x].T, 0.0)
    for j in range(NY - 1):
        frm_y = jnp.where(core == 0, j, NY - 1 - j)

        @pl.when(j < pos)
        def _():
            seq_copy(
                tot_send, tot_recv.at[j], tot_ss.at[0], tot_rs.at[j], dev(frm_y, x, core)
            ).wait_recv()
            state[...] = apply(state[...], tot_recv[j])

    xs = [None] * NX
    xs[0] = state[...]
    xs[2] = apply(xs[0], nodes[0])
    xs[1] = apply(xs[0], ef_recv[0])
    xs[3] = apply(xs[2], ef_recv[2])
    spot = 2 * (x % 2) + core
    for slot in range(NX):
        x_send[slot] = xs[slot].astype(bf16)
        to = jnp.where(core == 0, slot, NX - 1 - slot)
        local = hands & (to == x)

        @pl.when(jnp.logical_not(local))
        def _():
            seq_copy(x_send.at[slot], x_in.at[spot], x_ss, x_rs, dev(y, to, x // 2)).start()

        @pl.when(local)
        def _():
            x_in[spot] = x_send[slot]

    count(x_in, x_ss, x_rs, lambda c: c.wait_recv())
    for i in range(2):
        for role in range(2):
            at_first = x_in[2 * i + role]
            at_second = apply(at_first.astype(f32), first[i, role]).astype(bf16)
            wl[2 * core + i, role] = jnp.where(core == role, at_first, at_second)
            x_sib[i, role] = jnp.where(core == role, at_second, at_first)
    own_two = wl.at[pl.ds(2 * core, 2)]
    other_two = wl.at[pl.ds(2 * (1 - core), 2)]
    x_out = seq_copy(x_sib, own_two, xs_ss, xs_rs, sib)
    x_out.start()

    below, above = dev((y + NY - 1) % NY, x, core), dev((y + 1) % NY, x, core)
    src_at = [((y + i) % NY) * NC + core for i in range(NY)]
    low, high = pl.ds(0, W // 2), pl.ds(W // 2, W // 2)

    def ag_copy(half, off, kind, to):
        ref = raw_all.at[half, src_at[off]]
        if kind >= 2:
            ref = raw_all.at[half, src_at[off], low if kind == 2 else high]
        return seq_copy(ref, ref, ag_ss.at[half], ag_rs.at[half, kind], to)

    def sib_copy(half, off, cc):
        ref = raw_all.at[half, ((y + off) % NY) * NC + cc]
        return seq_copy(ref, ref, ag_ss.at[half], sib_rs.at[half, off], sib)

    rates = [rate_base * rate_ref[h] for h in range(NH)]
    for pair in range(2):
        half = (core + pair) % 2
        if pair == 1:
            seq_copy(other_two, other_two, xs_ss, xs_rs, sib).wait_recv()
        hs = [2 * half, 2 * half + 1]
        cut = pl.ds(pl.multiple_of(half * 2 * W, 2 * W), 2 * W)

        def two(ref):
            both = ref[:, cut]
            return [both[:, :W], both[:, W:]]

        kept = [[ref[h] for h in hs] for ref in (kf, invf, kbs, tks, tvs, ttks, ttzs)]
        us, gvs, raws = final_rows(
            *kept, None, two(q_ref), two(g_ref),
            [rate_base * rate_ref[h] for h in hs], [wl[h, 0] for h in hs], [wl[h, 1] for h in hs],
        )
        raw_all[half, src_me] = jnp.concatenate(raws, axis=1)
        ag_copy(half, 0, 0, above).start()
        ag_copy(half, 0, 1, below).start()
        sib_copy(half, 0, core).start()
        gv_ref[:, cut] = jnp.concatenate(gvs, axis=1)
        for i in range(2):
            ubs[hs[i]] = us[i]

    raw = jnp.concatenate([raw_all[0, src_me], raw_all[1, src_me]], axis=1)

    def part(off):
        rows = pl.ds(pl.multiple_of(z_at[off] * NH * W, NH * W), NH * W)
        out = nt(raw, kw_ref[rows, :])
        zs[off, 0] = out[:, :2 * W].astype(bf16)
        zs[off, 1] = out[:, 2 * W:].astype(bf16)

    def z_copy(way, n, half):
        off = 4 - n if way == 0 else (4 + n) % NZ
        to = (2 if n == 0 else 1) if way == 0 else (6 if n == 0 else 7)
        return head_copy(
            zs.at[off, half], zr.at[way, n, half], z_ss, z_rs.at[way, 2 * n + half], z_at[to]
        )

    def z_add(way, n, half):
        off = 4 - n if way == 0 else (4 + n) % NZ
        z_copy(way, n - 1, half).wait_recv()
        total = zs[off, half].astype(f32) + zr[way, n - 1, half].astype(f32)
        if n == 2 and half == way:
            z_copy(way, 0, half).wait_recv()
            total = total + zr[way, 0, half].astype(f32)
        zs[off, half] = total.astype(bf16)
        z_copy(way, n, half).start()

    def relay(half):
        ag_copy(half, 3, 0, sib).wait_recv()
        ag_copy(half, 3, 2, above).start()
        sib_copy(half, 3, core).start()
        ag_copy(half, 1, 1, sib).wait_recv()
        ag_copy(half, 1, 3, below).start()
        sib_copy(half, 1, core).start()

    def far(half):
        ag_copy(half, 2, 2, sib).wait_recv()
        ag_copy(half, 2, 3, sib).wait_recv()
        sib_copy(half, 2, core).start()

    def turn(src, c):
        cols = pl.ds(pl.multiple_of(src * W, W), W)
        for xx in range(NX):
            both = jnp.concatenate([tokcol[0, src, xx], tokcol[1, src, xx]], axis=0)
            tok_t[xx * W:xx * W + W, cols] = both.T
        return c

    x_at = [(x + i) % NX for i in range(NX)]
    right, left = dev(y, x_at[1], core), dev(y, x_at[3], core)

    def rs_copy(half, off, piece):
        rows = low if piece == 0 else high
        to_right = off == 1 or (off == 2 and piece == 0)
        return seq_copy(
            rs_s.at[half, off, rows], rs_r.at[half, off, rows], rs_ss.at[half],
            rs_rs.at[half, 2 * off + piece], right if to_right else left,
        )

    def products(half):
        for off in range(NY):
            sib_copy(half, off, 1 - core).wait_recv()
        out = mm(tok_t[...], raw_all[half].reshape(NC * NY * W, 2 * W))
        for xx in range(NX):
            psum[half, xx] = out[xx * W:xx * W + W]
        for off in (2, 1, 3):
            rs_s[half, off] = psum[half, x_at[off]].astype(bf16)
            if off == 2:
                rs_copy(half, 2, 0).start()
                rs_copy(half, 2, 1).start()
            else:
                rs_copy(half, off, 1 if off == 1 else 0).start()

    def rs_add(half):
        for off, piece in ((1, 0), (3, 1)):
            rows = slice(0, W // 2) if piece == 0 else slice(W // 2, W)
            rs_copy(half, 2, piece).wait_recv()
            rs_s[half, off, rows] = (
                psum[half, x_at[off], rows] + rs_r[half, 2, rows].astype(f32)
            ).astype(bf16)
            rs_copy(half, off, piece).start()

    def rs_end(half):
        for off in (1, 3):
            for piece in range(2):
                rs_copy(half, off, piece).wait_recv()
        gkw_ref[:, 2 * W * half:2 * W * (half + 1)] = (
            psum[half, x] + rs_r[half, 1].astype(f32) + rs_r[half, 3].astype(f32)
        )

    def grad_query(h):
        hs = slice(h * W, h * W + W)
        bi, bj = batch_of()
        g = g_ref[:, hs]
        lower = jnp.where(bi >= bj, nt(g, ubs[h]), 0.0).astype(bf16)
        gq_ref[:, hs] = (mm(g, wl[h, 0]) - rates[h] * mm(lower, kbs[h])).astype(bf16)

    part(3)
    z_copy(0, 1, 1).start()
    z_copy(0, 1, 0).start()
    part(5)
    z_copy(1, 1, 0).start()
    z_copy(1, 1, 1).start()
    part(4)
    z_copy(0, 0, 0).start()
    z_copy(1, 0, 1).start()
    part(2)
    part(6)
    relay(core)
    relay(1 - core)
    z_add(0, 2, 1)
    z_add(1, 2, 0)
    tz_in.wait_recv()
    lax.fori_loop(0, NC * NY, turn, 0)
    far(core)
    far(1 - core)
    z_add(0, 2, 0)
    z_add(1, 2, 1)
    part(1)
    part(7)
    products(0)
    products(1)
    z_add(0, 3, 1)
    z_add(1, 3, 0)
    part(0)
    rs_add(0)
    rs_add(1)
    z_add(0, 3, 0)
    z_add(1, 3, 1)
    for h in range(NH):
        grad_query(h)

    for half in range(2):
        z_copy(0, 3, half).wait_recv()
        z_copy(1, 3, half).wait_recv()
        gt_ref[:, 2 * W * half:2 * W * (half + 1)] = (
            zs[0, half].astype(f32) + zr[0, 3, half].astype(f32) + zr[1, 3, half].astype(f32)
        ).astype(bf16)
    rs_end(0)
    rs_end(1)

    sm_sum.wait_send()
    count(ef_recv, ef_ss, ef_rs, lambda c: c.wait_send())
    tok_sum.wait_send()
    tz_out.wait_send()
    for to_pos in range(1, NY):
        @pl.when(to_pos > pos)
        def _():
            seq_copy(tot_send, tot_recv.at[0], tot_ss.at[to_pos], tot_rs.at[0], sib).wait_send()
    count(x_in, x_ss, x_rs, lambda c: c.wait_send())
    x_out.wait_send()
    for half in range(2):
        ref = raw_all.at[half, pl.ds(0, 7)]
        seq_copy(ref, ref, ag_ss.at[half], sib_rs.at[half, 0], sib).wait_send()
        ref = rs_s.at[half, pl.ds(0, 3)]
        seq_copy(ref, ref, rs_ss.at[half], rs_rs.at[half, 0], sib).wait_send()
    some_z = zs.at[pl.ds(0, 7)]
    head_copy(some_z, some_z, z_ss, z_rs.at[0, 0], z_at[1]).wait_send()


def hand_over(a0, a1, a2, a3, b0, b1, b2, b3):
    for a, b in ((a0, b0), (a1, b1), (a2, b2), (a3, b3)):
        b[...] = a[...]


def per_device(tokens, key_weight, queries, values, grad_out, inner_start, head_rate):
    vmem = pl.BlockSpec(memory_space=pltpu.VMEM)
    smem = pl.BlockSpec(memory_space=pltpu.SMEM)
    anywhere = pl.BlockSpec(memory_space=pl.ANY)
    cols = NH * W
    sem = pltpu.SemaphoreType.DMA
    shapes = (
        jax.ShapeDtypeStruct((W, cols), bf16),
        jax.ShapeDtypeStruct((W, cols), f32),
        jax.ShapeDtypeStruct((W, cols), bf16),
        jax.ShapeDtypeStruct((W, cols), bf16),
    )
    outs = pl.pallas_call(
        kernel,
        out_shape=shapes,
        in_specs=[anywhere] * 6 + [smem],
        out_specs=(vmem,) * 4,
        scratch_shapes=[
            pltpu.VMEM(tokens.shape, bf16),
            pltpu.VMEM(key_weight.shape, bf16),
            pltpu.VMEM((W, cols), bf16),
            pltpu.VMEM((W, cols), bf16),
            pltpu.VMEM((W, cols), bf16),
            pltpu.VMEM((NH, W, W), f32),
            pltpu.VMEM((W, cols), f32),
            pltpu.VMEM((2, NC * NY, NX, W // 2, W), bf16),
            pltpu.VMEM((NX * W, NC * NY * W), bf16),
            pltpu.VMEM((NH, 2, 2 * W, W), bf16),
            pltpu.VMEM((2, 2, 2 * W, W), bf16),
            pltpu.VMEM((2, 2, 2 * W, W), bf16),
            pltpu.VMEM((2, 2, 2 * W, W), bf16),
            pltpu.VMEM((NX, 2 * W, W), bf16),
            pltpu.VMEM((2 * W, W), bf16),
            pltpu.VMEM((NY, 2 * W, W), bf16),
            pltpu.VMEM((2, 2 * W, W), f32),
            pltpu.VMEM((W, W), f32),
            pltpu.VMEM((NX, W, W), bf16),
            pltpu.VMEM((4, W, W), bf16),
            pltpu.VMEM((2, 2, W, W), bf16),
            pltpu.VMEM((NH, 2, W, W), bf16),
            pltpu.VMEM((NH, W, W), f32),
            pltpu.VMEM((NH, W, W), f32),
            pltpu.VMEM((NH, W, W), bf16),
            pltpu.VMEM((NH, W, W), bf16),
            pltpu.VMEM((NH, W, W), f32),
            pltpu.VMEM((NH, W, W), bf16),
            pltpu.VMEM((NH, W, W), f32),
            pltpu.VMEM((NH, W, W), bf16),
            pltpu.VMEM((2, NC * NY, W, 2 * W), bf16),
            pltpu.VMEM((2, NX, W, 2 * W), f32),
            pltpu.VMEM((2, NX, W, 2 * W), bf16),
            pltpu.VMEM((2, NX, W, 2 * W), bf16),
            pltpu.VMEM((NZ, 2, W, 2 * W), bf16),
            pltpu.VMEM((2, 4, 2, W, 2 * W), bf16),
            sem((5 + KW_PARTS,)),
            sem, sem, sem, sem,
            sem, sem, sem, sem,
            sem((NY,)), sem((NY,)),
            sem, sem, sem, sem,
            sem((2,)), sem((2, 4)), sem((2, 4)),
            sem((2,)), sem((2, 8)),
            sem, sem((2, 8)),
        ],
        compiler_params=pltpu.CompilerParams(
            collective_id=0, has_side_effects=True, vmem_limit_bytes=56 * 1024 * 1024
        ),
        name="layer",
    )(tokens, key_weight, queries, values, grad_out, inner_start, head_rate)
    return pl.pallas_call(
        hand_over,
        out_shape=shapes,
        in_specs=[vmem] * 4,
        out_specs=(vmem,) * 4,
        name="hand_over",
    )(*outs)


def solution(mesh):
    placed = (
        P("seq", None),
        P(None, "head"),
        P("seq", "head"),
        P("seq", "head"),
        P("seq", "head"),
        P("head", None, None),
        P("head"),
    )
    return jax.shard_map(
        per_device,
        mesh=mesh,
        in_specs=placed,
        out_specs=(P("seq", "head"),) * 4,
        check_vma=False,
    )
```

```python
import jax
import jax.numpy as jnp
from jax import lax
from jax.experimental import pallas as pl
from jax.experimental.pallas import tpu as pltpu
from jax.sharding import PartitionSpec as P

MESH = pl.DeviceIdType.MESH
bf16 = jnp.bfloat16
f32 = jnp.float32
rate_base = 0.1
norm_eps = 1e-06
W = 128
NH = 4
NX, NY, NC = 4, 4, 2
ROW = NX * NC
NZ = 8
KW_PARTS = 4


def mm(a, b):
    return lax.dot_general(a, b, (((1,), (0,)), ((), ())), preferred_element_type=f32)


def nt(a, b):
    return lax.dot_general(a, b, (((1,), (1,)), ((), ())), preferred_element_type=f32)


def tn(a, b):
    return lax.dot_general(a, b, (((0,), (0,)), ((), ())), preferred_element_type=f32)


def batch_of():
    rows = lax.broadcasted_iota(jnp.int32, (W, W), 0) >> 4
    cols = lax.broadcasted_iota(jnp.int32, (W, W), 1) >> 4
    return rows, cols


def local_maps(kraws, vs, qs, gs, rs):
    n = range(len(rs))
    bi, bj = batch_of()
    rows = lax.broadcasted_iota(jnp.int32, (W, W), 0)
    cols = lax.broadcasted_iota(jnp.int32, (W, W), 1)
    eye = jnp.where(rows == cols, 1.0, 0.0)
    near = ((bi >> 1) == (bj >> 1)) & (bi > bj)
    middle = ((bi >> 2) == (bj >> 2)) & ((bi >> 1) > (bj >> 1))
    distant = (bi >> 2) > (bj >> 2)
    invs = [lax.rsqrt(jnp.sum(kr * kr, axis=1, keepdims=True) + norm_eps) for kr in kraws]
    ks = [kraws[i] * invs[i] for i in n]
    kbs = [k.astype(bf16) for k in ks]
    ms = [rs[i] * nt(kbs[i], kbs[i]) for i in n]
    zs = [jnp.where(bi <= bj, nt(kbs[i], qs[i]), 0.0).astype(bf16) for i in n]
    ts = [eye - jnp.where(near, m, 0.0) for m in ms]
    for mask in (middle, distant):
        tbs = [t.astype(bf16) for t in ts]
        us = [mm(tbs[i], jnp.where(mask, ms[i], 0.0).astype(bf16)).astype(bf16) for i in n]
        ts = [ts[i] - mm(us[i], tbs[i]) for i in n]
    zs = [mm(zs[i], gs[i]).astype(bf16) for i in n]
    qgs = [tn(gs[i], qs[i]) for i in n]
    tbs = [t.astype(bf16) for t in ts]
    tks = [mm(tbs[i], kbs[i]).astype(bf16) for i in n]
    tvs = [mm(tbs[i], vs[i]) for i in n]
    ttzs = [tn(tbs[i], zs[i]) for i in n]
    ttks = [tn(tbs[i], kbs[i]).astype(bf16) for i in n]
    e0s = [(-rs[i] * tn(tks[i], kbs[i])).astype(bf16) for i in n]
    e1s = [(-rs[i] * tn(kbs[i], tks[i])).astype(bf16) for i in n]
    f0s = [(rs[i] * tn(tvs[i].astype(bf16), kbs[i])).astype(bf16) for i in n]
    f1s = [(qgs[i] - rs[i] * tn(ttzs[i].astype(bf16), kbs[i])).astype(bf16) for i in n]
    return ks, invs, kbs, tks, tvs, ttks, ttzs, e0s, f0s, e1s, f1s


def final_rows(k, inv, kb, tk, tv, ttk, ttz, v, q, g, r, w, l):
    n = range(len(r))
    bi, bj = batch_of()
    ubs = [(nt(tk[i], w[i]) - tv[i]).astype(bf16) for i in n]
    ys = [nt(ttk[i], l[i]) + ttz[i] for i in n]
    ybs = [y.astype(bf16) for y in ys]
    pms = [jnp.where(bi <= bj, nt(ubs[i], g[i]), 0.0).astype(bf16) for i in n]
    sms = [
        jnp.where(
            bi < bj, nt(ubs[i], ybs[i]), jnp.where(bi > bj, nt(ybs[i], ubs[i]), 0.0)
        ).astype(bf16)
        for i in n
    ]
    kas = [mm(ubs[i], l[i]) + mm(ybs[i], w[i]) for i in n]
    kas = [kas[i] + mm(pms[i], q[i]) for i in n]
    kas = [-r[i] * (kas[i] - r[i] * mm(sms[i], kb[i])) for i in n]
    alongs = [jnp.sum(k[i] * kas[i], axis=1, keepdims=True) for i in n]
    raws = [((kas[i] - k[i] * alongs[i]) * inv[i]).astype(bf16) for i in n]
    return ubs, [(r[i] * ys[i]).astype(bf16) for i in n], raws


def join(a, b):
    return a.astype(f32) + b.astype(f32) + mm(a.astype(bf16), b[:W].astype(bf16))


def apply(state, m):
    return state + mm(state.astype(bf16), m[:W].astype(bf16)) + m[W:].astype(f32)


def kernel(
    tok_hbm, kw_hbm, q_hbm, v_hbm, g_hbm, w0_hbm, rate_ref,
    gt_out, gkw_out, gq_out, gv_out,
    gt_ref, gkw_ref, gq_ref, gv_ref, tok_ref, kw_ref, q_ref, v_ref, g_ref, w0_ref, kraw_ref,
    tokcol, tok_t, maps, sib_maps, first, chip_maps, ef_recv, tot_send, tot_recv, nodes,
    state, x_send, x_in, x_sib, wl,
    kf, invf, kbs, tks, tvs, ttks, ttzs, ubs, raw_all, psum, rs_s, rs_r, zs, zr,
    in_s, out_s, tok_ss, tok_rs, tz_ss, tz_rs, sm_ss, sm_rs, ef_ss, ef_rs, tot_ss, tot_rs,
    x_ss, x_rs, xs_ss, xs_rs, ag_ss, ag_rs, sib_rs, rs_ss, rs_rs, z_ss, z_rs,
):
    me = lax.axis_index("seq")
    zme = lax.axis_index("head")
    y = me // ROW
    p = me % ROW
    x = p // NC
    core = p % NC
    sib = me + 1 - 2 * core
    hands = x // 2 == core

    def dev(yy, xx, cc):
        return (yy * NX + xx) * NC + cc

    def seq_copy(src, dst, ss, rs, to):
        return pltpu.make_async_remote_copy(
            src_ref=src, dst_ref=dst, send_sem=ss, recv_sem=rs,
            device_id={"seq": to}, device_id_type=MESH,
        )

    def head_copy(src, dst, ss, rs, to):
        return pltpu.make_async_remote_copy(
            src_ref=src, dst_ref=dst, send_sem=ss, recv_sem=rs,
            device_id={"head": to}, device_id_type=MESH,
        )

    deep = kw_ref.shape[0] // KW_PARTS
    loads = [pltpu.make_async_copy(tok_hbm, tok_ref, in_s.at[0])]
    for i in range(KW_PARTS):
        rows = pl.ds(i * deep, deep)
        loads.append(pltpu.make_async_copy(kw_hbm.at[rows], kw_ref.at[rows], in_s.at[1 + i]))
    for i, (src, dst) in enumerate(
        ((q_hbm, q_ref), (v_hbm, v_ref), (g_hbm, g_ref), (w0_hbm, w0_ref))
    ):
        loads.append(pltpu.make_async_copy(src, dst, in_s.at[1 + KW_PARTS + i]))
    for load in loads:
        load.start()

    leave = [
        pltpu.make_async_copy(src, dst, out_s.at[i])
        for i, (src, dst) in enumerate(
            ((gt_ref, gt_out), (gkw_ref, gkw_out), (gq_ref, gq_out), (gv_ref, gv_out))
        )
    ]

    barrier = pltpu.get_barrier_semaphore()

    def greet_seq(to):
        pl.semaphore_signal(barrier, inc=1, device_id={"seq": to}, device_id_type=MESH)

    for i in range(1, ROW):
        greet_seq(y * ROW + (p + i) % ROW)
    for i in range(1, NY):
        for cc in range(NC):
            greet_seq(dev((y + i) % NY, x, cc))
    z_at = [(zme + i) % NZ for i in range(NZ)]
    for i in (1, 2, 6, 7):
        pl.semaphore_signal(
            barrier, inc=1, device_id={"head": z_at[i]}, device_id_type=MESH
        )
    partners = ROW - 1 + NC * (NY - 1) + 4

    loads[0].wait()
    kraw = None
    for i in range(KW_PARTS):
        loads[1 + i].wait()
        rows = slice(i * deep, (i + 1) * deep)
        prod = mm(tok_ref[:, rows], kw_ref[rows, :])
        kraw = prod if kraw is None else kraw + prod
    kraw_ref[...] = kraw
    for load in loads[1 + KW_PARTS:]:
        load.wait()
    zp = zme % 2
    half_rows = pl.ds(pl.multiple_of(zp * (W // 2), W // 2), W // 2)
    src_me = y * NC + core

    def tok_cols(yy, xx, cc):
        return pl.ds(pl.multiple_of(dev(yy, xx, cc) * W, W), W)

    def tok_start(yy, cc):
        for xx in range(NX):
            seq_copy(
                tok_ref.at[half_rows, tok_cols(yy, xx, cc)], tokcol.at[zp, src_me, xx],
                tok_ss, tok_rs, dev(yy, x, cc),
            ).start()

    sm_out = seq_copy(maps.at[pl.ds(2 * (1 - core), 2)], sib_maps, sm_ss, sm_rs, sib)
    pl.semaphore_wait(barrier, partners)
    for cc in range(NC):
        tok_start((y + 2) % NY, cc)
    tok_start((y + 1) % NY, core)
    tok_start((y + 1) % NY, 1 - core)
    for cc in range(NC):
        tok_start((y + 3) % NY, cc)
    tok_start(y, 1 - core)
    for pair in range(2):
        base = 2 * ((1 - core + pair) % 2)
        cut = pl.ds(pl.multiple_of(base * W, 2 * W), 2 * W)

        def two(ref):
            both = ref[:, cut]
            return [both[:, :W], both[:, W:]]

        found = local_maps(
            two(kraw_ref), two(v_ref), two(q_ref), two(g_ref),
            [rate_base * rate_ref[base + i] for i in range(2)],
        )
        for i in range(2):
            h = base + i
            k, inv, kb, tk, tv, ttk, ttz, e0, f0, e1, f1 = [each[i] for each in found]
            maps[h, 0, :W] = e0
            maps[h, 0, W:] = f0
            maps[h, 1, :W] = e1
            maps[h, 1, W:] = f1
            kf[h] = k
            invf[h] = jnp.broadcast_to(inv, (W, W))
            kbs[h] = kb
            tks[h] = tk
            tvs[h] = tv
            ttks[h] = ttk
            ttzs[h] = ttz
        if pair == 0:
            sm_out.start()

    sm_sum = seq_copy(sib_maps, sib_maps, sm_ss, sm_rs, sib)
    sm_sum.wait_recv()
    i_far = jnp.where(hands, 1 - x % 2, x % 2)
    for step in range(2):
        i = i_far if step == 0 else 1 - i_far
        h = 2 * core + i
        for role in range(2):
            here, there = maps[h, role], sib_maps[i, role]
            mine_first = core == role
            one = jnp.where(mine_first, here, there)
            first[i, role] = one
            chip_maps[i, role] = join(one, jnp.where(mine_first, there, here)).astype(bf16)
            slot = x if role == 0 else NX - 1 - x
            local = (x == h) & (core == role)

            @pl.when(jnp.logical_not(local))
            def _():
                seq_copy(
                    chip_maps.at[i, role], ef_recv.at[slot], ef_ss, ef_rs, dev(y, h, role)
                ).start()

            @pl.when(local)
            def _():
                ef_recv[slot] = chip_maps[i, role]

    for xx in range(NX):
        tokcol[zp, src_me, xx] = tok_ref[half_rows, tok_cols(y, xx, core)]
    tok_all = tokcol.at[0, pl.ds(0, 2 * NY - 1)]
    tok_sum = seq_copy(tok_all, tok_all, tok_ss, tok_rs, sib)
    tz_out = head_copy(tokcol.at[zp], tokcol.at[zp], tz_ss, tz_rs, zme + 1 - 2 * zp)
    tz_in = head_copy(tokcol.at[1 - zp], tokcol.at[1 - zp], tz_ss, tz_rs, zme + 1 - 2 * zp)

    def count(ref, ss, rs, act):
        few = ref.at[pl.ds(0, NX - 1)]

        @pl.when(hands)
        def _():
            act(seq_copy(few, few, ss, rs, sib))

        @pl.when(jnp.logical_not(hands))
        def _():
            act(seq_copy(ref, ref, ss, rs, sib))

    count(ef_recv, ef_ss, ef_rs, lambda c: c.wait_recv())
    for i in range(2):
        nodes[i] = join(ef_recv[2 * i], ef_recv[2 * i + 1])
    tot_send[...] = join(nodes[0], nodes[1]).astype(bf16)

    pos = jnp.where(core == 0, y, NY - 1 - y)
    for to_pos in range(NY - 1, 0, -1):
        to_y = jnp.where(core == 0, to_pos, NY - 1 - to_pos)

        @pl.when(to_pos > pos)
        def _():
            seq_copy(
                tot_send, tot_recv.at[pos], tot_ss.at[to_pos], tot_rs.at[pos],
                dev(to_y, x, core),
            ).start()

    tok_sum.wait_recv()
    tz_out.start()

    state[...] = jnp.where(core == 0, w0_ref[x].T, 0.0)
    for j in range(NY - 1):
        frm_y = jnp.where(core == 0, j, NY - 1 - j)

        @pl.when(j < pos)
        def _():
            seq_copy(
                tot_send, tot_recv.at[j], tot_ss.at[0], tot_rs.at[j], dev(frm_y, x, core)
            ).wait_recv()
            state[...] = apply(state[...], tot_recv[j])

    xs = [None] * NX
    xs[0] = state[...]
    xs[2] = apply(xs[0], nodes[0])
    xs[1] = apply(xs[0], ef_recv[0])
    xs[3] = apply(xs[2], ef_recv[2])
    spot = 2 * (x % 2) + core
    for slot in range(NX):
        x_send[slot] = xs[slot].astype(bf16)
        to = jnp.where(core == 0, slot, NX - 1 - slot)
        local = hands & (to == x)

        @pl.when(jnp.logical_not(local))
        def _():
            seq_copy(x_send.at[slot], x_in.at[spot], x_ss, x_rs, dev(y, to, x // 2)).start()

        @pl.when(local)
        def _():
            x_in[spot] = x_send[slot]

    count(x_in, x_ss, x_rs, lambda c: c.wait_recv())
    for i in range(2):
        for role in range(2):
            at_first = x_in[2 * i + role]
            at_second = apply(at_first.astype(f32), first[i, role]).astype(bf16)
            wl[2 * core + i, role] = jnp.where(core == role, at_first, at_second)
            x_sib[i, role] = jnp.where(core == role, at_second, at_first)
    own_two = wl.at[pl.ds(2 * core, 2)]
    other_two = wl.at[pl.ds(2 * (1 - core), 2)]
    x_out = seq_copy(x_sib, own_two, xs_ss, xs_rs, sib)
    x_out.start()

    below, above = dev((y + NY - 1) % NY, x, core), dev((y + 1) % NY, x, core)
    src_at = [((y + i) % NY) * NC + core for i in range(NY)]
    low, high = pl.ds(0, W // 2), pl.ds(W // 2, W // 2)

    def ag_copy(half, off, kind, to):
        rows = low if kind in (0, 2, 5) else high
        ref = raw_all.at[half, src_at[off], rows]
        return seq_copy(ref, ref, ag_ss.at[half], ag_rs.at[half, kind], to)

    def sib_copy(half, off, cc):
        ref = raw_all.at[half, ((y + off) % NY) * NC + cc]
        return seq_copy(ref, ref, ag_ss.at[half], sib_rs.at[half, off], sib)

    rates = [rate_base * rate_ref[h] for h in range(NH)]
    for pair in range(2):
        half = (core + pair) % 2
        if pair == 1:
            seq_copy(other_two, other_two, xs_ss, xs_rs, sib).wait_recv()
        hs = [2 * half, 2 * half + 1]
        cut = pl.ds(pl.multiple_of(half * 2 * W, 2 * W), 2 * W)

        def two(ref):
            both = ref[:, cut]
            return [both[:, :W], both[:, W:]]

        kept = [[ref[h] for h in hs] for ref in (kf, invf, kbs, tks, tvs, ttks, ttzs)]
        us, gvs, raws = final_rows(
            *kept, None, two(q_ref), two(g_ref),
            [rate_base * rate_ref[h] for h in hs], [wl[h, 0] for h in hs], [wl[h, 1] for h in hs],
        )
        raw_all[half, src_me] = jnp.concatenate(raws, axis=1)
        ag_copy(half, 0, 0, above).start()
        ag_copy(half, 0, 1, below).start()
        ag_copy(half, 0, 4, above).start()
        ag_copy(half, 0, 5, below).start()
        sib_copy(half, 0, core).start()
        gv_ref[:, cut] = jnp.concatenate(gvs, axis=1)
        for i in range(2):
            ubs[hs[i]] = us[i]

    raw = jnp.concatenate([raw_all[0, src_me], raw_all[1, src_me]], axis=1)

    def part(off):
        rows = pl.ds(pl.multiple_of(z_at[off] * NH * W, NH * W), NH * W)
        out = nt(raw, kw_ref[rows, :])
        for piece in range(NH):
            zs[off, piece] = out[:, piece * W:piece * W + W].astype(bf16)

    def z_far(way):
        both = pl.ds(2 * way, 2)
        return head_copy(
            zs.at[4, both], zr.at[way, 0, both], z_ss, z_rs.at[way, 0],
            z_at[2 if way == 0 else 6],
        )

    def z_copy(way, n, piece):
        off = 4 - n if way == 0 else 4 + n
        return head_copy(
            zs.at[off, piece], zr.at[way, n, piece], z_ss, z_rs.at[way, NH * n + piece],
            z_at[1 if way == 0 else 7],
        )

    def z_add(n, early, i):
        for way in range(2):
            piece = 2 * (1 - way if early else way) + i
            off = 4 - n if way == 0 else 4 + n
            z_copy(way, n - 1, piece).wait_recv()
            total = zs[off, piece].astype(f32) + zr[way, n - 1, piece].astype(f32)
            if n == 2 and not early:
                if i == 0:
                    z_far(way).wait_recv()
                total = total + zr[way, 0, piece].astype(f32)
            zs[off, piece] = total.astype(bf16)
            z_copy(way, n, piece).start()

    def relay(half):
        ag_copy(half, 3, 0, sib).wait_recv()
        ag_copy(half, 3, 2, above).start()
        ag_copy(half, 1, 1, sib).wait_recv()
        ag_copy(half, 1, 3, below).start()

    def near(half):
        ag_copy(half, 3, 4, sib).wait_recv()
        sib_copy(half, 3, core).start()
        ag_copy(half, 1, 5, sib).wait_recv()
        sib_copy(half, 1, core).start()

    def far(half):
        ag_copy(half, 2, 2, sib).wait_recv()
        ag_copy(half, 2, 3, sib).wait_recv()
        sib_copy(half, 2, core).start()

    def turn(src, c):
        cols = pl.ds(pl.multiple_of(src * W, W), W)
        for xx in range(NX):
            both = jnp.concatenate([tokcol[0, src, xx], tokcol[1, src, xx]], axis=0)
            tok_t[xx * W:xx * W + W, cols] = both.T
        return c

    x_at = [(x + i) % NX for i in range(NX)]
    right, left = dev(y, x_at[1], core), dev(y, x_at[3], core)

    def rs_copy(half, off, piece):
        rows = low if piece == 0 else high
        to_right = off == 1 or (off == 2 and piece == 0)
        return seq_copy(
            rs_s.at[half, off, rows], rs_r.at[half, off, rows], rs_ss.at[half],
            rs_rs.at[half, 2 * off + piece], right if to_right else left,
        )

    def products(half):
        for off in range(NY):
            sib_copy(half, off, 1 - core).wait_recv()
        out = mm(tok_t[...], raw_all[half].reshape(NC * NY * W, 2 * W))
        for xx in range(NX):
            psum[half, xx] = out[xx * W:xx * W + W]
        for off in (2, 1, 3):
            rs_s[half, off] = psum[half, x_at[off]].astype(bf16)
            if off == 2:
                rs_copy(half, 2, 0).start()
                rs_copy(half, 2, 1).start()
            else:
                rs_copy(half, off, 1 if off == 1 else 0).start()

    def rs_add(half):
        for off, piece in ((1, 0), (3, 1)):
            rows = slice(0, W // 2) if piece == 0 else slice(W // 2, W)
            rs_copy(half, 2, piece).wait_recv()
            rs_s[half, off, rows] = (
                psum[half, x_at[off], rows] + rs_r[half, 2, rows].astype(f32)
            ).astype(bf16)
            rs_copy(half, off, piece).start()

    def rs_end(half):
        for off in (1, 3):
            for piece in range(2):
                rs_copy(half, off, piece).wait_recv()
        gkw_ref[:, 2 * W * half:2 * W * (half + 1)] = (
            psum[half, x] + rs_r[half, 1].astype(f32) + rs_r[half, 3].astype(f32)
        )

    def grad_query(h):
        hs = slice(h * W, h * W + W)
        bi, bj = batch_of()
        g = g_ref[:, hs]
        lower = jnp.where(bi >= bj, nt(g, ubs[h]), 0.0).astype(bf16)
        gq_ref[:, hs] = (mm(g, wl[h, 0]) - rates[h] * mm(lower, kbs[h])).astype(bf16)

    part(3)
    z_copy(0, 1, 2).start()
    z_copy(0, 1, 3).start()
    part(5)
    z_copy(1, 1, 0).start()
    z_copy(1, 1, 1).start()
    part(4)
    z_far(0).start()
    z_far(1).start()
    for i in range(2):
        z_copy(0, 1, i).start()
        z_copy(1, 1, 2 + i).start()
    part(2)
    part(6)
    relay(core)
    relay(1 - core)
    near(core)
    z_add(2, True, 0)
    z_add(2, True, 1)
    near(1 - core)
    part(1)
    part(7)
    tz_in.wait_recv()
    lax.fori_loop(0, NC * NY, turn, 0)
    far(core)
    far(1 - core)
    products(0)
    z_add(2, False, 0)
    products(1)
    z_add(2, False, 1)
    z_add(3, True, 0)
    z_add(3, True, 1)
    z_add(3, False, 0)
    z_add(3, False, 1)
    part(0)
    rs_add(0)
    rs_add(1)
    leave[3].start()
    for h in range(NH):
        grad_query(h)
    leave[2].start()

    for piece in (2, 3, 0, 1):
        z_copy(0, 3, piece).wait_recv()
        z_copy(1, 3, piece).wait_recv()
        gt_ref[:, piece * W:piece * W + W] = (
            zs[0, piece].astype(f32) + zr[0, 3, piece].astype(f32) + zr[1, 3, piece].astype(f32)
        ).astype(bf16)
    leave[0].start()
    rs_end(0)
    rs_end(1)
    leave[1].start()

    sm_sum.wait_send()
    count(ef_recv, ef_ss, ef_rs, lambda c: c.wait_send())
    tok_sum.wait_send()
    tz_out.wait_send()
    for to_pos in range(1, NY):
        @pl.when(to_pos > pos)
        def _():
            seq_copy(tot_send, tot_recv.at[0], tot_ss.at[to_pos], tot_rs.at[0], sib).wait_send()
    count(x_in, x_ss, x_rs, lambda c: c.wait_send())
    x_out.wait_send()
    for half in range(2):
        ref = raw_all.at[half, pl.ds(0, 7)]
        seq_copy(ref, ref, ag_ss.at[half], sib_rs.at[half, 0], sib).wait_send()
        ref = rs_s.at[half, pl.ds(0, 3)]
        seq_copy(ref, ref, rs_ss.at[half], rs_rs.at[half, 0], sib).wait_send()
    some_z = zs.at[pl.ds(0, 7)]
    head_copy(some_z, some_z, z_ss, z_rs.at[0, 0], z_at[1]).wait_send()
    for copy in leave:
        copy.wait()


def hand_over(a0, a1, a2, a3, b0, b1, b2, b3, v0, v1, v2, v3, sems):
    ins = [
        pltpu.make_async_copy(a, v, sems.at[i])
        for i, (a, v) in enumerate(((a0, v0), (a1, v1), (a2, v2), (a3, v3)))
    ]
    outs = [
        pltpu.make_async_copy(v, b, sems.at[4 + i])
        for i, (v, b) in enumerate(((v0, b0), (v1, b1), (v2, b2), (v3, b3)))
    ]
    for copy in ins:
        copy.start()
    for copy, after in zip(ins, outs):
        copy.wait()
        after.start()
    for copy in outs:
        copy.wait()


def per_device(tokens, key_weight, queries, values, grad_out, inner_start, head_rate):
    vmem = pl.BlockSpec(memory_space=pltpu.VMEM)
    smem = pl.BlockSpec(memory_space=pltpu.SMEM)
    anywhere = pl.BlockSpec(memory_space=pl.ANY)
    cols = NH * W
    sem = pltpu.SemaphoreType.DMA
    shapes = (
        jax.ShapeDtypeStruct((W, cols), bf16),
        jax.ShapeDtypeStruct((W, cols), f32),
        jax.ShapeDtypeStruct((W, cols), bf16),
        jax.ShapeDtypeStruct((W, cols), bf16),
    )
    outs = pl.pallas_call(
        kernel,
        out_shape=shapes,
        in_specs=[anywhere] * 6 + [smem],
        out_specs=(anywhere,) * 4,
        scratch_shapes=[
            *[pltpu.VMEM(a.shape, a.dtype) for a in shapes],
            pltpu.VMEM(tokens.shape, bf16),
            pltpu.VMEM(key_weight.shape, bf16),
            pltpu.VMEM((W, cols), bf16),
            pltpu.VMEM((W, cols), bf16),
            pltpu.VMEM((W, cols), bf16),
            pltpu.VMEM((NH, W, W), f32),
            pltpu.VMEM((W, cols), f32),
            pltpu.VMEM((2, NC * NY, NX, W // 2, W), bf16),
            pltpu.VMEM((NX * W, NC * NY * W), bf16),
            pltpu.VMEM((NH, 2, 2 * W, W), bf16),
            pltpu.VMEM((2, 2, 2 * W, W), bf16),
            pltpu.VMEM((2, 2, 2 * W, W), bf16),
            pltpu.VMEM((2, 2, 2 * W, W), bf16),
            pltpu.VMEM((NX, 2 * W, W), bf16),
            pltpu.VMEM((2 * W, W), bf16),
            pltpu.VMEM((NY, 2 * W, W), bf16),
            pltpu.VMEM((2, 2 * W, W), f32),
            pltpu.VMEM((W, W), f32),
            pltpu.VMEM((NX, W, W), bf16),
            pltpu.VMEM((4, W, W), bf16),
            pltpu.VMEM((2, 2, W, W), bf16),
            pltpu.VMEM((NH, 2, W, W), bf16),
            pltpu.VMEM((NH, W, W), f32),
            pltpu.VMEM((NH, W, W), f32),
            pltpu.VMEM((NH, W, W), bf16),
            pltpu.VMEM((NH, W, W), bf16),
            pltpu.VMEM((NH, W, W), f32),
            pltpu.VMEM((NH, W, W), bf16),
            pltpu.VMEM((NH, W, W), f32),
            pltpu.VMEM((NH, W, W), bf16),
            pltpu.VMEM((2, NC * NY, W, 2 * W), bf16),
            pltpu.VMEM((2, NX, W, 2 * W), f32),
            pltpu.VMEM((2, NX, W, 2 * W), bf16),
            pltpu.VMEM((2, NX, W, 2 * W), bf16),
            pltpu.VMEM((NZ, NH, W, W), bf16),
            pltpu.VMEM((2, 4, NH, W, W), bf16),
            sem((5 + KW_PARTS,)),
            sem((4,)),
            sem, sem, sem, sem,
            sem, sem, sem, sem,
            sem((NY,)), sem((NY,)),
            sem, sem, sem, sem,
            sem((2,)), sem((2, 6)), sem((2, 4)),
            sem((2,)), sem((2, 8)),
            sem, sem((2, 4 * NH)),
        ],
        compiler_params=pltpu.CompilerParams(
            collective_id=0, has_side_effects=True, vmem_limit_bytes=56 * 1024 * 1024
        ),
        name="layer",
    )(tokens, key_weight, queries, values, grad_out, inner_start, head_rate)
    return pl.pallas_call(
        hand_over,
        out_shape=shapes,
        in_specs=[anywhere] * 4,
        out_specs=(anywhere,) * 4,
        scratch_shapes=[pltpu.VMEM(a.shape, a.dtype) for a in shapes] + [sem((8,))],
        name="hand_over",
    )(*outs)


def solution(mesh):
    placed = (
        P("seq", None),
        P(None, "head"),
        P("seq", "head"),
        P("seq", "head"),
        P("seq", "head"),
        P("head", None, None),
        P("head"),
    )
    return jax.shard_map(
        per_device,
        mesh=mesh,
        in_specs=placed,
        out_specs=(P("seq", "head"),) * 4,
        check_vma=False,
    )
```

```python
import jax
import jax.numpy as jnp
from jax import lax
from jax.experimental import pallas as pl
from jax.experimental.pallas import tpu as pltpu
from jax.sharding import PartitionSpec as P

MESH = pl.DeviceIdType.MESH
bf16 = jnp.bfloat16
f32 = jnp.float32
rate_base = 0.1
norm_eps = 1e-06
W = 128
NH = 4
NX, NY, NC = 4, 4, 2
ROW = NX * NC
NZ = 8
KW_PARTS = 4


def mm(a, b):
    return lax.dot_general(a, b, (((1,), (0,)), ((), ())), preferred_element_type=f32)


def nt(a, b):
    return lax.dot_general(a, b, (((1,), (1,)), ((), ())), preferred_element_type=f32)


def tn(a, b):
    return lax.dot_general(a, b, (((0,), (0,)), ((), ())), preferred_element_type=f32)


def batch_of():
    rows = lax.broadcasted_iota(jnp.int32, (W, W), 0) >> 4
    cols = lax.broadcasted_iota(jnp.int32, (W, W), 1) >> 4
    return rows, cols


def local_maps(kraws, vs, qs, gs, rs):
    n = range(len(rs))
    bi, bj = batch_of()
    rows = lax.broadcasted_iota(jnp.int32, (W, W), 0)
    cols = lax.broadcasted_iota(jnp.int32, (W, W), 1)
    eye = jnp.where(rows == cols, 1.0, 0.0)
    near = ((bi >> 1) == (bj >> 1)) & (bi > bj)
    middle = ((bi >> 2) == (bj >> 2)) & ((bi >> 1) > (bj >> 1))
    distant = (bi >> 2) > (bj >> 2)
    invs = [lax.rsqrt(jnp.sum(kr * kr, axis=1, keepdims=True) + norm_eps) for kr in kraws]
    ks = [kraws[i] * invs[i] for i in n]
    kbs = [k.astype(bf16) for k in ks]
    ms = [rs[i] * nt(kbs[i], kbs[i]) for i in n]
    zs = [jnp.where(bi <= bj, nt(kbs[i], qs[i]), 0.0).astype(bf16) for i in n]
    ts = [eye - jnp.where(near, m, 0.0) for m in ms]
    for mask in (middle, distant):
        tbs = [t.astype(bf16) for t in ts]
        us = [mm(tbs[i], jnp.where(mask, ms[i], 0.0).astype(bf16)).astype(bf16) for i in n]
        ts = [ts[i] - mm(us[i], tbs[i]) for i in n]
    zs = [mm(zs[i], gs[i]).astype(bf16) for i in n]
    qgs = [tn(gs[i], qs[i]) for i in n]
    tbs = [t.astype(bf16) for t in ts]
    tks = [mm(tbs[i], kbs[i]).astype(bf16) for i in n]
    tvs = [mm(tbs[i], vs[i]) for i in n]
    ttzs = [tn(tbs[i], zs[i]) for i in n]
    ttks = [tn(tbs[i], kbs[i]).astype(bf16) for i in n]
    e0s = [(-rs[i] * tn(tks[i], kbs[i])).astype(bf16) for i in n]
    e1s = [(-rs[i] * tn(kbs[i], tks[i])).astype(bf16) for i in n]
    f0s = [(rs[i] * tn(tvs[i].astype(bf16), kbs[i])).astype(bf16) for i in n]
    f1s = [(qgs[i] - rs[i] * tn(ttzs[i].astype(bf16), kbs[i])).astype(bf16) for i in n]
    return ks, invs, kbs, tks, tvs, ttks, ttzs, e0s, f0s, e1s, f1s


def final_rows(k, inv, kb, tk, tv, ttk, ttz, v, q, g, r, w, l):
    n = range(len(r))
    bi, bj = batch_of()
    ubs = [(nt(tk[i], w[i]) - tv[i]).astype(bf16) for i in n]
    ys = [nt(ttk[i], l[i]) + ttz[i] for i in n]
    ybs = [y.astype(bf16) for y in ys]
    pms = [jnp.where(bi <= bj, nt(ubs[i], g[i]), 0.0).astype(bf16) for i in n]
    sms = [
        jnp.where(
            bi < bj, nt(ubs[i], ybs[i]), jnp.where(bi > bj, nt(ybs[i], ubs[i]), 0.0)
        ).astype(bf16)
        for i in n
    ]
    kas = [mm(ubs[i], l[i]) + mm(ybs[i], w[i]) for i in n]
    kas = [kas[i] + mm(pms[i], q[i]) for i in n]
    kas = [-r[i] * (kas[i] - r[i] * mm(sms[i], kb[i])) for i in n]
    alongs = [jnp.sum(k[i] * kas[i], axis=1, keepdims=True) for i in n]
    raws = [((kas[i] - k[i] * alongs[i]) * inv[i]).astype(bf16) for i in n]
    return ubs, [(r[i] * ys[i]).astype(bf16) for i in n], raws


def join(a, b):
    return a.astype(f32) + b.astype(f32) + mm(a.astype(bf16), b[:W].astype(bf16))


def apply(state, m):
    return state + mm(state.astype(bf16), m[:W].astype(bf16)) + m[W:].astype(f32)


def kernel(
    tok_hbm, kw_hbm, q_hbm, v_hbm, g_hbm, w0_hbm, rate_ref,
    gt_out, gkw_out, gq_out, gv_out,
    gt_ref, gkw_ref, gq_ref, gv_ref, tok_ref, kw_ref, q_ref, v_ref, g_ref, w0_ref, kraw_ref,
    tokcol, tok_t, maps, sib_maps, first, chip_maps, ef_recv, tot_send, tot_recv, nodes,
    state, x_send, x_in, x_sib, wl,
    kf, invf, kbs, tks, tvs, ttks, ttzs, ubs, raw_all, psum, rs_s, rs_r, zs, zr,
    in_s, out_s, tok_ss, tok_rs, tz_ss, tz_rs, sm_ss, sm_rs, ef_ss, ef_rs, tot_ss, tot_rs,
    x_ss, x_rs, xs_ss, xs_rs, ag_ss, ag_rs, sib_rs, rs_ss, rs_rs, z_ss, z_rs,
):
    me = lax.axis_index("seq")
    zme = lax.axis_index("head")
    y = me // ROW
    p = me % ROW
    x = p // NC
    core = p % NC
    sib = me + 1 - 2 * core
    hands = x // 2 == core

    def dev(yy, xx, cc):
        return (yy * NX + xx) * NC + cc

    def seq_copy(src, dst, ss, rs, to):
        return pltpu.make_async_remote_copy(
            src_ref=src, dst_ref=dst, send_sem=ss, recv_sem=rs,
            device_id={"seq": to}, device_id_type=MESH,
        )

    def head_copy(src, dst, ss, rs, to):
        return pltpu.make_async_remote_copy(
            src_ref=src, dst_ref=dst, send_sem=ss, recv_sem=rs,
            device_id={"head": to}, device_id_type=MESH,
        )

    deep = kw_ref.shape[0] // KW_PARTS
    loads = [pltpu.make_async_copy(tok_hbm, tok_ref, in_s.at[0])]
    for i in range(KW_PARTS):
        rows = pl.ds(i * deep, deep)
        loads.append(pltpu.make_async_copy(kw_hbm.at[rows], kw_ref.at[rows], in_s.at[1 + i]))
    for i, (src, dst) in enumerate(
        ((q_hbm, q_ref), (v_hbm, v_ref), (g_hbm, g_ref), (w0_hbm, w0_ref))
    ):
        loads.append(pltpu.make_async_copy(src, dst, in_s.at[1 + KW_PARTS + i]))
    for load in loads:
        load.start()

    leave = [
        pltpu.make_async_copy(src, dst, out_s.at[i])
        for i, (src, dst) in enumerate(
            ((gt_ref, gt_out), (gkw_ref, gkw_out), (gq_ref, gq_out), (gv_ref, gv_out))
        )
    ]

    barrier = pltpu.get_barrier_semaphore()

    def greet_seq(to):
        pl.semaphore_signal(barrier, inc=1, device_id={"seq": to}, device_id_type=MESH)

    for i in range(1, ROW):
        greet_seq(y * ROW + (p + i) % ROW)
    for i in range(1, NY):
        for cc in range(NC):
            greet_seq(dev((y + i) % NY, x, cc))
    z_at = [(zme + i) % NZ for i in range(NZ)]
    for i in (1, 2, 6, 7):
        pl.semaphore_signal(
            barrier, inc=1, device_id={"head": z_at[i]}, device_id_type=MESH
        )
    partners = ROW - 1 + NC * (NY - 1) + 4

    loads[0].wait()
    kraw = None
    for i in range(KW_PARTS):
        loads[1 + i].wait()
        rows = slice(i * deep, (i + 1) * deep)
        prod = mm(tok_ref[:, rows], kw_ref[rows, :])
        kraw = prod if kraw is None else kraw + prod
    kraw_ref[...] = kraw
    for load in loads[1 + KW_PARTS:]:
        load.wait()
    zp = zme % 2
    half_rows = pl.ds(pl.multiple_of(zp * (W // 2), W // 2), W // 2)
    src_me = y * NC + core

    def tok_cols(yy, xx, cc):
        return pl.ds(pl.multiple_of(dev(yy, xx, cc) * W, W), W)

    def tok_start(yy, cc):
        for xx in range(NX):
            seq_copy(
                tok_ref.at[half_rows, tok_cols(yy, xx, cc)], tokcol.at[zp, src_me, xx],
                tok_ss, tok_rs, dev(yy, x, cc),
            ).start()

    sm_out = seq_copy(maps.at[pl.ds(2 * (1 - core), 2)], sib_maps, sm_ss, sm_rs, sib)
    pl.semaphore_wait(barrier, partners)
    for cc in range(NC):
        tok_start((y + 2) % NY, cc)
    tok_start((y + 1) % NY, core)
    tok_start((y + 1) % NY, 1 - core)
    for cc in range(NC):
        tok_start((y + 3) % NY, cc)
    tok_start(y, 1 - core)
    for pair in range(2):
        base = 2 * ((1 - core + pair) % 2)
        cut = pl.ds(pl.multiple_of(base * W, 2 * W), 2 * W)

        def two(ref):
            both = ref[:, cut]
            return [both[:, :W], both[:, W:]]

        found = local_maps(
            two(kraw_ref), two(v_ref), two(q_ref), two(g_ref),
            [rate_base * rate_ref[base + i] for i in range(2)],
        )
        for i in range(2):
            h = base + i
            k, inv, kb, tk, tv, ttk, ttz, e0, f0, e1, f1 = [each[i] for each in found]
            maps[h, 0, :W] = e0
            maps[h, 0, W:] = f0
            maps[h, 1, :W] = e1
            maps[h, 1, W:] = f1
            kf[h] = k
            invf[h] = jnp.broadcast_to(inv, (W, W))
            kbs[h] = kb
            tks[h] = tk
            tvs[h] = tv
            ttks[h] = ttk
            ttzs[h] = ttz
        if pair == 0:
            sm_out.start()

    sm_sum = seq_copy(sib_maps, sib_maps, sm_ss, sm_rs, sib)
    sm_sum.wait_recv()
    i_far = jnp.where(hands, 1 - x % 2, x % 2)
    for step in range(2):
        i = i_far if step == 0 else 1 - i_far
        h = 2 * core + i
        for role in range(2):
            here, there = maps[h, role], sib_maps[i, role]
            mine_first = core == role
            one = jnp.where(mine_first, here, there)
            first[i, role] = one
            chip_maps[i, role] = join(one, jnp.where(mine_first, there, here)).astype(bf16)
            slot = x if role == 0 else NX - 1 - x
            local = (x == h) & (core == role)

            @pl.when(jnp.logical_not(local))
            def _():
                seq_copy(
                    chip_maps.at[i, role], ef_recv.at[slot], ef_ss, ef_rs, dev(y, h, role)
                ).start()

            @pl.when(local)
            def _():
                ef_recv[slot] = chip_maps[i, role]

    for xx in range(NX):
        tokcol[zp, src_me, xx] = tok_ref[half_rows, tok_cols(y, xx, core)]
    tok_all = tokcol.at[0, pl.ds(0, 2 * NY - 1)]
    tok_sum = seq_copy(tok_all, tok_all, tok_ss, tok_rs, sib)
    tz_out = head_copy(tokcol.at[zp], tokcol.at[zp], tz_ss, tz_rs, zme + 1 - 2 * zp)
    tz_in = head_copy(tokcol.at[1 - zp], tokcol.at[1 - zp], tz_ss, tz_rs, zme + 1 - 2 * zp)

    def count(ref, ss, rs, act):
        few = ref.at[pl.ds(0, NX - 1)]

        @pl.when(hands)
        def _():
            act(seq_copy(few, few, ss, rs, sib))

        @pl.when(jnp.logical_not(hands))
        def _():
            act(seq_copy(ref, ref, ss, rs, sib))

    count(ef_recv, ef_ss, ef_rs, lambda c: c.wait_recv())
    for i in range(2):
        nodes[i] = join(ef_recv[2 * i], ef_recv[2 * i + 1])
    tot_send[...] = join(nodes[0], nodes[1]).astype(bf16)

    pos = jnp.where(core == 0, y, NY - 1 - y)
    for to_pos in range(NY - 1, 0, -1):
        to_y = jnp.where(core == 0, to_pos, NY - 1 - to_pos)

        @pl.when(to_pos > pos)
        def _():
            seq_copy(
                tot_send, tot_recv.at[pos], tot_ss.at[to_pos], tot_rs.at[pos],
                dev(to_y, x, core),
            ).start()

    tok_sum.wait_recv()
    tz_out.start()

    state[...] = jnp.where(core == 0, w0_ref[x].T, 0.0)
    for j in range(NY - 1):
        frm_y = jnp.where(core == 0, j, NY - 1 - j)

        @pl.when(j < pos)
        def _():
            seq_copy(
                tot_send, tot_recv.at[j], tot_ss.at[0], tot_rs.at[j], dev(frm_y, x, core)
            ).wait_recv()
            state[...] = apply(state[...], tot_recv[j])

    xs = [None] * NX
    xs[0] = state[...]
    xs[2] = apply(xs[0], nodes[0])
    xs[1] = apply(xs[0], ef_recv[0])
    xs[3] = apply(xs[2], ef_recv[2])
    spot = 2 * (x % 2) + core
    for slot in range(NX):
        x_send[slot] = xs[slot].astype(bf16)
        to = jnp.where(core == 0, slot, NX - 1 - slot)
        local = hands & (to == x)

        @pl.when(jnp.logical_not(local))
        def _():
            seq_copy(x_send.at[slot], x_in.at[spot], x_ss, x_rs, dev(y, to, x // 2)).start()

        @pl.when(local)
        def _():
            x_in[spot] = x_send[slot]

    count(x_in, x_ss, x_rs, lambda c: c.wait_recv())
    for i in range(2):
        for role in range(2):
            at_first = x_in[2 * i + role]
            at_second = apply(at_first.astype(f32), first[i, role]).astype(bf16)
            wl[2 * core + i, role] = jnp.where(core == role, at_first, at_second)
            x_sib[i, role] = jnp.where(core == role, at_second, at_first)
    own_two = wl.at[pl.ds(2 * core, 2)]
    other_two = wl.at[pl.ds(2 * (1 - core), 2)]
    x_out = seq_copy(x_sib, own_two, xs_ss, xs_rs, sib)
    x_out.start()

    below, above = dev((y + NY - 1) % NY, x, core), dev((y + 1) % NY, x, core)
    src_at = [((y + i) % NY) * NC + core for i in range(NY)]
    low, high = pl.ds(0, W // 2), pl.ds(W // 2, W // 2)

    def ag_copy(half, off, kind, to):
        rows = low if kind in (0, 2, 5) else high
        ref = raw_all.at[half, src_at[off], rows]
        return seq_copy(ref, ref, ag_ss.at[half], ag_rs.at[half, kind], to)

    def sib_copy(half, off, cc):
        ref = raw_all.at[half, ((y + off) % NY) * NC + cc]
        return seq_copy(ref, ref, ag_ss.at[half], sib_rs.at[half, off], sib)

    rates = [rate_base * rate_ref[h] for h in range(NH)]
    for pair in range(2):
        half = (core + pair) % 2
        if pair == 1:
            seq_copy(other_two, other_two, xs_ss, xs_rs, sib).wait_recv()
        hs = [2 * half, 2 * half + 1]
        cut = pl.ds(pl.multiple_of(half * 2 * W, 2 * W), 2 * W)

        def two(ref):
            both = ref[:, cut]
            return [both[:, :W], both[:, W:]]

        kept = [[ref[h] for h in hs] for ref in (kf, invf, kbs, tks, tvs, ttks, ttzs)]
        us, gvs, raws = final_rows(
            *kept, None, two(q_ref), two(g_ref),
            [rate_base * rate_ref[h] for h in hs], [wl[h, 0] for h in hs], [wl[h, 1] for h in hs],
        )
        raw_all[half, src_me] = jnp.concatenate(raws, axis=1)
        ag_copy(half, 0, 0, above).start()
        ag_copy(half, 0, 1, below).start()
        ag_copy(half, 0, 4, above).start()
        ag_copy(half, 0, 5, below).start()
        sib_copy(half, 0, core).start()
        gv_ref[:, cut] = jnp.concatenate(gvs, axis=1)
        for i in range(2):
            ubs[hs[i]] = us[i]

    raw = jnp.concatenate([raw_all[0, src_me], raw_all[1, src_me]], axis=1)

    def part(off):
        rows = pl.ds(pl.multiple_of(z_at[off] * NH * W, NH * W), NH * W)
        out = nt(raw, kw_ref[rows, :])
        for piece in range(NH):
            zs[off, piece] = out[:, piece * W:piece * W + W].astype(bf16)

    def z_far(way):
        both = pl.ds(2 * way, 2)
        return head_copy(
            zs.at[4, both], zr.at[way, 0, both], z_ss, z_rs.at[way, 0],
            z_at[2 if way == 0 else 6],
        )

    def z_copy(way, n, piece):
        off = 4 - n if way == 0 else 4 + n
        return head_copy(
            zs.at[off, piece], zr.at[way, n, piece], z_ss, z_rs.at[way, NH * n + piece],
            z_at[1 if way == 0 else 7],
        )

    def z_add(n, early, i):
        for way in range(2):
            piece = 2 * (1 - way if early else way) + i
            off = 4 - n if way == 0 else 4 + n
            z_copy(way, n - 1, piece).wait_recv()
            total = zs[off, piece].astype(f32) + zr[way, n - 1, piece].astype(f32)
            if n == 2 and not early:
                if i == 0:
                    z_far(way).wait_recv()
                total = total + zr[way, 0, piece].astype(f32)
            zs[off, piece] = total.astype(bf16)
            z_copy(way, n, piece).start()

    def relay(half):
        ag_copy(half, 3, 0, sib).wait_recv()
        ag_copy(half, 3, 2, above).start()
        ag_copy(half, 1, 1, sib).wait_recv()
        ag_copy(half, 1, 3, below).start()

    def near(half):
        ag_copy(half, 3, 4, sib).wait_recv()
        sib_copy(half, 3, core).start()
        ag_copy(half, 1, 5, sib).wait_recv()
        sib_copy(half, 1, core).start()

    def far(half):
        ag_copy(half, 2, 2, sib).wait_recv()
        ag_copy(half, 2, 3, sib).wait_recv()
        sib_copy(half, 2, core).start()

    def turn(src, c):
        cols = pl.ds(pl.multiple_of(src * W, W), W)
        for xx in range(NX):
            both = jnp.concatenate([tokcol[0, src, xx], tokcol[1, src, xx]], axis=0)
            tok_t[xx * W:xx * W + W, cols] = both.T
        return c

    x_at = [(x + i) % NX for i in range(NX)]
    right, left = dev(y, x_at[1], core), dev(y, x_at[3], core)

    def rs_copy(half, off, piece):
        rows = low if piece == 0 else high
        to_right = off == 1 or (off == 2 and piece == 0)
        return seq_copy(
            rs_s.at[half, off, rows], rs_r.at[half, off, rows], rs_ss.at[half],
            rs_rs.at[half, 2 * off + piece], right if to_right else left,
        )

    def products(half):
        for off in range(NY):
            sib_copy(half, off, 1 - core).wait_recv()
        out = mm(tok_t[...], raw_all[half].reshape(NC * NY * W, 2 * W))
        for xx in range(NX):
            psum[half, xx] = out[xx * W:xx * W + W]
        for off in (2, 1, 3):
            rs_s[half, off] = psum[half, x_at[off]].astype(bf16)
            if off == 2:
                rs_copy(half, 2, 0).start()
                rs_copy(half, 2, 1).start()
            else:
                rs_copy(half, off, 1 if off == 1 else 0).start()

    def rs_add(half):
        for off, piece in ((1, 0), (3, 1)):
            rows = slice(0, W // 2) if piece == 0 else slice(W // 2, W)
            rs_copy(half, 2, piece).wait_recv()
            rs_s[half, off, rows] = (
                psum[half, x_at[off], rows] + rs_r[half, 2, rows].astype(f32)
            ).astype(bf16)
            rs_copy(half, off, piece).start()

    def rs_end(half):
        for off in (1, 3):
            for piece in range(2):
                rs_copy(half, off, piece).wait_recv()
        gkw_ref[:, 2 * W * half:2 * W * (half + 1)] = (
            psum[half, x] + rs_r[half, 1].astype(f32) + rs_r[half, 3].astype(f32)
        )

    def grad_query(h):
        hs = slice(h * W, h * W + W)
        bi, bj = batch_of()
        g = g_ref[:, hs]
        lower = jnp.where(bi >= bj, nt(g, ubs[h]), 0.0).astype(bf16)
        gq_ref[:, hs] = (mm(g, wl[h, 0]) - rates[h] * mm(lower, kbs[h])).astype(bf16)

    part(3)
    z_copy(0, 1, 2).start()
    z_copy(0, 1, 3).start()
    part(5)
    z_copy(1, 1, 0).start()
    z_copy(1, 1, 1).start()
    part(4)
    z_far(0).start()
    z_far(1).start()
    for i in range(2):
        z_copy(0, 1, i).start()
        z_copy(1, 1, 2 + i).start()
    part(2)
    part(6)
    relay(core)
    near(core)
    relay(1 - core)
    near(1 - core)
    tz_in.wait_recv()
    lax.fori_loop(0, NC * NY, turn, 0)
    z_add(2, True, 0)
    z_add(2, True, 1)
    far(core)
    far(1 - core)
    products(core)
    z_add(2, False, 0)
    products(1 - core)
    z_add(2, False, 1)
    part(1)
    part(7)
    z_add(3, True, 0)
    z_add(3, True, 1)
    rs_add(core)
    z_add(3, False, 0)
    z_add(3, False, 1)
    rs_add(1 - core)
    part(0)
    leave[3].start()
    for h in range(NH):
        grad_query(h)
    leave[2].start()

    for piece in (2, 3, 0, 1):
        z_copy(0, 3, piece).wait_recv()
        z_copy(1, 3, piece).wait_recv()
        gt_ref[:, piece * W:piece * W + W] = (
            zs[0, piece].astype(f32) + zr[0, 3, piece].astype(f32) + zr[1, 3, piece].astype(f32)
        ).astype(bf16)
    leave[0].start()
    rs_end(0)
    rs_end(1)
    leave[1].start()

    sm_sum.wait_send()
    count(ef_recv, ef_ss, ef_rs, lambda c: c.wait_send())
    tok_sum.wait_send()
    tz_out.wait_send()
    for to_pos in range(1, NY):
        @pl.when(to_pos > pos)
        def _():
            seq_copy(tot_send, tot_recv.at[0], tot_ss.at[to_pos], tot_rs.at[0], sib).wait_send()
    count(x_in, x_ss, x_rs, lambda c: c.wait_send())
    x_out.wait_send()
    for half in range(2):
        ref = raw_all.at[half, pl.ds(0, 7)]
        seq_copy(ref, ref, ag_ss.at[half], sib_rs.at[half, 0], sib).wait_send()
        ref = rs_s.at[half, pl.ds(0, 3)]
        seq_copy(ref, ref, rs_ss.at[half], rs_rs.at[half, 0], sib).wait_send()
    some_z = zs.at[pl.ds(0, 7)]
    head_copy(some_z, some_z, z_ss, z_rs.at[0, 0], z_at[1]).wait_send()
    for copy in leave:
        copy.wait()


def hand_over(a0, a1, a2, a3, b0, b1, b2, b3, v0, v1, v2, v3, sems):
    ins = [
        pltpu.make_async_copy(a, v, sems.at[i])
        for i, (a, v) in enumerate(((a0, v0), (a1, v1), (a2, v2), (a3, v3)))
    ]
    outs = [
        pltpu.make_async_copy(v, b, sems.at[4 + i])
        for i, (v, b) in enumerate(((v0, b0), (v1, b1), (v2, b2), (v3, b3)))
    ]
    for copy in ins:
        copy.start()
    for copy, after in zip(ins, outs):
        copy.wait()
        after.start()
    for copy in outs:
        copy.wait()


def per_device(tokens, key_weight, queries, values, grad_out, inner_start, head_rate):
    vmem = pl.BlockSpec(memory_space=pltpu.VMEM)
    smem = pl.BlockSpec(memory_space=pltpu.SMEM)
    anywhere = pl.BlockSpec(memory_space=pl.ANY)
    cols = NH * W
    sem = pltpu.SemaphoreType.DMA
    shapes = (
        jax.ShapeDtypeStruct((W, cols), bf16),
        jax.ShapeDtypeStruct((W, cols), f32),
        jax.ShapeDtypeStruct((W, cols), bf16),
        jax.ShapeDtypeStruct((W, cols), bf16),
    )
    outs = pl.pallas_call(
        kernel,
        out_shape=shapes,
        in_specs=[anywhere] * 6 + [smem],
        out_specs=(anywhere,) * 4,
        scratch_shapes=[
            *[pltpu.VMEM(a.shape, a.dtype) for a in shapes],
            pltpu.VMEM(tokens.shape, bf16),
            pltpu.VMEM(key_weight.shape, bf16),
            pltpu.VMEM((W, cols), bf16),
            pltpu.VMEM((W, cols), bf16),
            pltpu.VMEM((W, cols), bf16),
            pltpu.VMEM((NH, W, W), f32),
            pltpu.VMEM((W, cols), f32),
            pltpu.VMEM((2, NC * NY, NX, W // 2, W), bf16),
            pltpu.VMEM((NX * W, NC * NY * W), bf16),
            pltpu.VMEM((NH, 2, 2 * W, W), bf16),
            pltpu.VMEM((2, 2, 2 * W, W), bf16),
            pltpu.VMEM((2, 2, 2 * W, W), bf16),
            pltpu.VMEM((2, 2, 2 * W, W), bf16),
            pltpu.VMEM((NX, 2 * W, W), bf16),
            pltpu.VMEM((2 * W, W), bf16),
            pltpu.VMEM((NY, 2 * W, W), bf16),
            pltpu.VMEM((2, 2 * W, W), f32),
            pltpu.VMEM((W, W), f32),
            pltpu.VMEM((NX, W, W), bf16),
            pltpu.VMEM((4, W, W), bf16),
            pltpu.VMEM((2, 2, W, W), bf16),
            pltpu.VMEM((NH, 2, W, W), bf16),
            pltpu.VMEM((NH, W, W), f32),
            pltpu.VMEM((NH, W, W), f32),
            pltpu.VMEM((NH, W, W), bf16),
            pltpu.VMEM((NH, W, W), bf16),
            pltpu.VMEM((NH, W, W), f32),
            pltpu.VMEM((NH, W, W), bf16),
            pltpu.VMEM((NH, W, W), f32),
            pltpu.VMEM((NH, W, W), bf16),
            pltpu.VMEM((2, NC * NY, W, 2 * W), bf16),
            pltpu.VMEM((2, NX, W, 2 * W), f32),
            pltpu.VMEM((2, NX, W, 2 * W), bf16),
            pltpu.VMEM((2, NX, W, 2 * W), bf16),
            pltpu.VMEM((NZ, NH, W, W), bf16),
            pltpu.VMEM((2, 4, NH, W, W), bf16),
            sem((5 + KW_PARTS,)),
            sem((4,)),
            sem, sem, sem, sem,
            sem, sem, sem, sem,
            sem((NY,)), sem((NY,)),
            sem, sem, sem, sem,
            sem((2,)), sem((2, 6)), sem((2, 4)),
            sem((2,)), sem((2, 8)),
            sem, sem((2, 4 * NH)),
        ],
        compiler_params=pltpu.CompilerParams(
            collective_id=0, has_side_effects=True, vmem_limit_bytes=56 * 1024 * 1024
        ),
        name="layer",
    )(tokens, key_weight, queries, values, grad_out, inner_start, head_rate)
    return pl.pallas_call(
        hand_over,
        out_shape=shapes,
        in_specs=[anywhere] * 4,
        out_specs=(anywhere,) * 4,
        scratch_shapes=[pltpu.VMEM(a.shape, a.dtype) for a in shapes] + [sem((8,))],
        name="hand_over",
    )(*outs)


def solution(mesh):
    placed = (
        P("seq", None),
        P(None, "head"),
        P("seq", "head"),
        P("seq", "head"),
        P("seq", "head"),
        P("head", None, None),
        P("head"),
    )
    return jax.shard_map(
        per_device,
        mesh=mesh,
        in_specs=placed,
        out_specs=(P("seq", "head"),) * 4,
        check_vma=False,
    )
```

```python
import jax
import jax.numpy as jnp
from jax import lax
from jax.experimental import pallas as pl
from jax.experimental.pallas import tpu as pltpu
from jax.sharding import PartitionSpec as P

MESH = pl.DeviceIdType.MESH
bf16 = jnp.bfloat16
f32 = jnp.float32
rate_base = 0.1
norm_eps = 1e-06
W = 128
NH = 4
NX, NY, NC = 4, 4, 2
ROW = NX * NC
NZ = 8
KW_PARTS = 4


def mm(a, b):
    return lax.dot_general(a, b, (((1,), (0,)), ((), ())), preferred_element_type=f32)


def nt(a, b):
    return lax.dot_general(a, b, (((1,), (1,)), ((), ())), preferred_element_type=f32)


def tn(a, b):
    return lax.dot_general(a, b, (((0,), (0,)), ((), ())), preferred_element_type=f32)


def batch_of():
    rows = lax.broadcasted_iota(jnp.int32, (W, W), 0) >> 4
    cols = lax.broadcasted_iota(jnp.int32, (W, W), 1) >> 4
    return rows, cols


def local_maps(kraws, vs, qs, gs, rs):
    n = range(len(rs))
    bi, bj = batch_of()
    rows = lax.broadcasted_iota(jnp.int32, (W, W), 0)
    cols = lax.broadcasted_iota(jnp.int32, (W, W), 1)
    eye = jnp.where(rows == cols, 1.0, 0.0)
    near = ((bi >> 1) == (bj >> 1)) & (bi > bj)
    middle = ((bi >> 2) == (bj >> 2)) & ((bi >> 1) > (bj >> 1))
    distant = (bi >> 2) > (bj >> 2)
    invs = [lax.rsqrt(jnp.sum(kr * kr, axis=1, keepdims=True) + norm_eps) for kr in kraws]
    ks = [kraws[i] * invs[i] for i in n]
    kbs = [k.astype(bf16) for k in ks]
    ms = [rs[i] * nt(kbs[i], kbs[i]) for i in n]
    zs = [jnp.where(bi <= bj, nt(kbs[i], qs[i]), 0.0).astype(bf16) for i in n]
    ts = [eye - jnp.where(near, m, 0.0) for m in ms]
    for mask in (middle, distant):
        tbs = [t.astype(bf16) for t in ts]
        us = [mm(tbs[i], jnp.where(mask, ms[i], 0.0).astype(bf16)).astype(bf16) for i in n]
        ts = [ts[i] - mm(us[i], tbs[i]) for i in n]
    zs = [mm(zs[i], gs[i]).astype(bf16) for i in n]
    qgs = [tn(gs[i], qs[i]) for i in n]
    tbs = [t.astype(bf16) for t in ts]
    tks = [mm(tbs[i], kbs[i]).astype(bf16) for i in n]
    tvs = [mm(tbs[i], vs[i]) for i in n]
    ttzs = [tn(tbs[i], zs[i]) for i in n]
    ttks = [tn(tbs[i], kbs[i]).astype(bf16) for i in n]
    e0s = [(-rs[i] * tn(tks[i], kbs[i])).astype(bf16) for i in n]
    e1s = [(-rs[i] * tn(kbs[i], tks[i])).astype(bf16) for i in n]
    f0s = [(rs[i] * tn(tvs[i].astype(bf16), kbs[i])).astype(bf16) for i in n]
    f1s = [(qgs[i] - rs[i] * tn(ttzs[i].astype(bf16), kbs[i])).astype(bf16) for i in n]
    return ks, invs, kbs, tks, tvs, ttks, ttzs, e0s, f0s, e1s, f1s


def final_rows(k, inv, kb, tk, tv, ttk, ttz, v, q, g, r, w, l):
    n = range(len(r))
    bi, bj = batch_of()
    ubs = [(nt(tk[i], w[i]) - tv[i]).astype(bf16) for i in n]
    ys = [nt(ttk[i], l[i]) + ttz[i] for i in n]
    ybs = [y.astype(bf16) for y in ys]
    pms = [jnp.where(bi <= bj, nt(ubs[i], g[i]), 0.0).astype(bf16) for i in n]
    sms = [
        jnp.where(
            bi < bj, nt(ubs[i], ybs[i]), jnp.where(bi > bj, nt(ybs[i], ubs[i]), 0.0)
        ).astype(bf16)
        for i in n
    ]
    kas = [mm(ubs[i], l[i]) + mm(ybs[i], w[i]) for i in n]
    kas = [kas[i] + mm(pms[i], q[i]) for i in n]
    kas = [-r[i] * (kas[i] - r[i] * mm(sms[i], kb[i])) for i in n]
    alongs = [jnp.sum(k[i] * kas[i], axis=1, keepdims=True) for i in n]
    raws = [((kas[i] - k[i] * alongs[i]) * inv[i]).astype(bf16) for i in n]
    return ubs, [(r[i] * ys[i]).astype(bf16) for i in n], raws


def join(a, b):
    return a.astype(f32) + b.astype(f32) + mm(a.astype(bf16), b[:W].astype(bf16))


def apply(state, m):
    return state + mm(state.astype(bf16), m[:W].astype(bf16)) + m[W:].astype(f32)


def kernel(
    tok_hbm, kw_hbm, q_hbm, v_hbm, g_hbm, w0_hbm, rate_ref,
    gt_out, gkw_out, gq_out, gv_out,
    gt_ref, gkw_ref, gq_ref, gv_ref, tok_ref, kw_ref, q_ref, v_ref, g_ref, w0_ref, kraw_ref,
    tokcol, tok_t, maps, sib_maps, first, chip_maps, ef_recv, tot_send, tot_recv, nodes,
    state, x_send, x_in, x_sib, wl,
    kf, invf, kbs, tks, tvs, ttks, ttzs, ubs, raw_all, psum, rs_s, rs_r, zs, zr,
    in_s, out_s, tok_ss, tok_rs, tz_ss, tz_rs, sm_ss, sm_rs, ef_ss, ef_rs, tot_ss, tot_rs,
    x_ss, x_rs, xs_ss, xs_rs, ag_ss, ag_rs, sib_rs, rs_ss, rs_rs, z_ss, z_rs,
):
    me = lax.axis_index("seq")
    zme = lax.axis_index("head")
    y = me // ROW
    p = me % ROW
    x = p // NC
    core = p % NC
    sib = me + 1 - 2 * core
    hands = x // 2 == core

    def dev(yy, xx, cc):
        return (yy * NX + xx) * NC + cc

    def seq_copy(src, dst, ss, rs, to):
        return pltpu.make_async_remote_copy(
            src_ref=src, dst_ref=dst, send_sem=ss, recv_sem=rs,
            device_id={"seq": to}, device_id_type=MESH,
        )

    def head_copy(src, dst, ss, rs, to):
        return pltpu.make_async_remote_copy(
            src_ref=src, dst_ref=dst, send_sem=ss, recv_sem=rs,
            device_id={"head": to}, device_id_type=MESH,
        )

    deep = kw_ref.shape[0] // KW_PARTS
    loads = [pltpu.make_async_copy(tok_hbm, tok_ref, in_s.at[0])]
    for i in range(KW_PARTS):
        rows = pl.ds(i * deep, deep)
        loads.append(pltpu.make_async_copy(kw_hbm.at[rows], kw_ref.at[rows], in_s.at[1 + i]))
    for i, (src, dst) in enumerate(
        ((q_hbm, q_ref), (v_hbm, v_ref), (g_hbm, g_ref), (w0_hbm, w0_ref))
    ):
        loads.append(pltpu.make_async_copy(src, dst, in_s.at[1 + KW_PARTS + i]))
    for load in loads:
        load.start()

    leave = [
        pltpu.make_async_copy(src, dst, out_s.at[i])
        for i, (src, dst) in enumerate(
            ((gt_ref, gt_out), (gkw_ref, gkw_out), (gq_ref, gq_out), (gv_ref, gv_out))
        )
    ]

    barrier = pltpu.get_barrier_semaphore()

    def greet_seq(to):
        pl.semaphore_signal(barrier, inc=1, device_id={"seq": to}, device_id_type=MESH)

    for i in range(1, ROW):
        greet_seq(y * ROW + (p + i) % ROW)
    for i in range(1, NY):
        for cc in range(NC):
            greet_seq(dev((y + i) % NY, x, cc))
    z_at = [(zme + i) % NZ for i in range(NZ)]
    for i in (1, 2, 6, 7):
        pl.semaphore_signal(
            barrier, inc=1, device_id={"head": z_at[i]}, device_id_type=MESH
        )
    partners = ROW - 1 + NC * (NY - 1) + 4

    loads[0].wait()
    kraw = None
    for i in range(KW_PARTS):
        loads[1 + i].wait()
        rows = slice(i * deep, (i + 1) * deep)
        prod = mm(tok_ref[:, rows], kw_ref[rows, :])
        kraw = prod if kraw is None else kraw + prod
    kraw_ref[...] = kraw
    for load in loads[1 + KW_PARTS:]:
        load.wait()
    zp = zme % 2
    half_rows = pl.ds(pl.multiple_of(zp * (W // 2), W // 2), W // 2)
    src_me = y * NC + core

    def tok_cols(yy, xx, cc):
        return pl.ds(pl.multiple_of(dev(yy, xx, cc) * W, W), W)

    def tok_start(yy, cc):
        for xx in range(NX):
            seq_copy(
                tok_ref.at[half_rows, tok_cols(yy, xx, cc)], tokcol.at[zp, src_me, xx],
                tok_ss, tok_rs, dev(yy, x, cc),
            ).start()

    sm_out = seq_copy(maps.at[pl.ds(2 * (1 - core), 2)], sib_maps, sm_ss, sm_rs, sib)
    pl.semaphore_wait(barrier, partners)
    for cc in range(NC):
        tok_start((y + 2) % NY, cc)
    tok_start((y + 1) % NY, core)
    tok_start((y + 1) % NY, 1 - core)
    for cc in range(NC):
        tok_start((y + 3) % NY, cc)
    tok_start(y, 1 - core)
    for pair in range(2):
        base = 2 * ((1 - core + pair) % 2)
        cut = pl.ds(pl.multiple_of(base * W, 2 * W), 2 * W)

        def two(ref):
            both = ref[:, cut]
            return [both[:, :W], both[:, W:]]

        found = local_maps(
            two(kraw_ref), two(v_ref), two(q_ref), two(g_ref),
            [rate_base * rate_ref[base + i] for i in range(2)],
        )
        for i in range(2):
            h = base + i
            k, inv, kb, tk, tv, ttk, ttz, e0, f0, e1, f1 = [each[i] for each in found]
            maps[h, 0, :W] = e0
            maps[h, 0, W:] = f0
            maps[h, 1, :W] = e1
            maps[h, 1, W:] = f1
            kf[h] = k
            invf[h] = jnp.broadcast_to(inv, (W, W))
            kbs[h] = kb
            tks[h] = tk
            tvs[h] = tv
            ttks[h] = ttk
            ttzs[h] = ttz
        if pair == 0:
            sm_out.start()

    sm_sum = seq_copy(sib_maps, sib_maps, sm_ss, sm_rs, sib)
    sm_sum.wait_recv()
    i_far = jnp.where(hands, 1 - x % 2, x % 2)
    for step in range(2):
        i = i_far if step == 0 else 1 - i_far
        h = 2 * core + i
        for role in range(2):
            here, there = maps[h, role], sib_maps[i, role]
            mine_first = core == role
            one = jnp.where(mine_first, here, there)
            first[i, role] = one
            chip_maps[i, role] = join(one, jnp.where(mine_first, there, here)).astype(bf16)
            slot = x if role == 0 else NX - 1 - x
            local = (x == h) & (core == role)

            @pl.when(jnp.logical_not(local))
            def _():
                seq_copy(
                    chip_maps.at[i, role], ef_recv.at[slot], ef_ss, ef_rs, dev(y, h, role)
                ).start()

            @pl.when(local)
            def _():
                ef_recv[slot] = chip_maps[i, role]

    for xx in range(NX):
        tokcol[zp, src_me, xx] = tok_ref[half_rows, tok_cols(y, xx, core)]
    tok_all = tokcol.at[0, pl.ds(0, 2 * NY - 1)]
    tok_sum = seq_copy(tok_all, tok_all, tok_ss, tok_rs, sib)
    tz_out = head_copy(tokcol.at[zp], tokcol.at[zp], tz_ss, tz_rs, zme + 1 - 2 * zp)
    tz_in = head_copy(tokcol.at[1 - zp], tokcol.at[1 - zp], tz_ss, tz_rs, zme + 1 - 2 * zp)

    def count(ref, ss, rs, act):
        few = ref.at[pl.ds(0, NX - 1)]

        @pl.when(hands)
        def _():
            act(seq_copy(few, few, ss, rs, sib))

        @pl.when(jnp.logical_not(hands))
        def _():
            act(seq_copy(ref, ref, ss, rs, sib))

    count(ef_recv, ef_ss, ef_rs, lambda c: c.wait_recv())
    for i in range(2):
        nodes[i] = join(ef_recv[2 * i], ef_recv[2 * i + 1])
    tot_send[...] = join(nodes[0], nodes[1]).astype(bf16)

    pos = jnp.where(core == 0, y, NY - 1 - y)
    for to_pos in range(NY - 1, 0, -1):
        to_y = jnp.where(core == 0, to_pos, NY - 1 - to_pos)

        @pl.when(to_pos > pos)
        def _():
            seq_copy(
                tot_send, tot_recv.at[pos], tot_ss.at[to_pos], tot_rs.at[pos],
                dev(to_y, x, core),
            ).start()

    tok_sum.wait_recv()
    tz_out.start()

    state[...] = jnp.where(core == 0, w0_ref[x].T, 0.0)
    for j in range(NY - 1):
        frm_y = jnp.where(core == 0, j, NY - 1 - j)

        @pl.when(j < pos)
        def _():
            seq_copy(
                tot_send, tot_recv.at[j], tot_ss.at[0], tot_rs.at[j], dev(frm_y, x, core)
            ).wait_recv()
            state[...] = apply(state[...], tot_recv[j])

    xs = [None] * NX
    xs[0] = state[...]
    xs[2] = apply(xs[0], nodes[0])
    xs[1] = apply(xs[0], ef_recv[0])
    xs[3] = apply(xs[2], ef_recv[2])
    spot = 2 * (x % 2) + core
    for slot in range(NX):
        x_send[slot] = xs[slot].astype(bf16)
        to = jnp.where(core == 0, slot, NX - 1 - slot)
        local = hands & (to == x)

        @pl.when(jnp.logical_not(local))
        def _():
            seq_copy(x_send.at[slot], x_in.at[spot], x_ss, x_rs, dev(y, to, x // 2)).start()

        @pl.when(local)
        def _():
            x_in[spot] = x_send[slot]

    count(x_in, x_ss, x_rs, lambda c: c.wait_recv())
    for i in range(2):
        for role in range(2):
            at_first = x_in[2 * i + role]
            at_second = apply(at_first.astype(f32), first[i, role]).astype(bf16)
            wl[2 * core + i, role] = jnp.where(core == role, at_first, at_second)
            x_sib[i, role] = jnp.where(core == role, at_second, at_first)
    own_two = wl.at[pl.ds(2 * core, 2)]
    other_two = wl.at[pl.ds(2 * (1 - core), 2)]
    x_out = seq_copy(x_sib, own_two, xs_ss, xs_rs, sib)
    x_out.start()

    below, above = dev((y + NY - 1) % NY, x, core), dev((y + 1) % NY, x, core)
    src_at = [((y + i) % NY) * NC + core for i in range(NY)]
    low, high = pl.ds(0, W // 2), pl.ds(W // 2, W // 2)

    def ag_copy(half, off, kind, to):
        rows = low if kind in (0, 2, 5) else high
        ref = raw_all.at[half, src_at[off], rows]
        return seq_copy(ref, ref, ag_ss.at[half], ag_rs.at[half, kind], to)

    def sib_copy(half, off, cc):
        ref = raw_all.at[half, ((y + off) % NY) * NC + cc]
        return seq_copy(ref, ref, ag_ss.at[half], sib_rs.at[half, off], sib)

    rates = [rate_base * rate_ref[h] for h in range(NH)]
    for pair in range(2):
        half = (core + pair) % 2
        if pair == 1:
            seq_copy(other_two, other_two, xs_ss, xs_rs, sib).wait_recv()
        hs = [2 * half, 2 * half + 1]
        cut = pl.ds(pl.multiple_of(half * 2 * W, 2 * W), 2 * W)

        def two(ref):
            both = ref[:, cut]
            return [both[:, :W], both[:, W:]]

        kept = [[ref[h] for h in hs] for ref in (kf, invf, kbs, tks, tvs, ttks, ttzs)]
        us, gvs, raws = final_rows(
            *kept, None, two(q_ref), two(g_ref),
            [rate_base * rate_ref[h] for h in hs], [wl[h, 0] for h in hs], [wl[h, 1] for h in hs],
        )
        raw_all[half, src_me] = jnp.concatenate(raws, axis=1)
        ag_copy(half, 0, 0, above).start()
        ag_copy(half, 0, 1, below).start()
        ag_copy(half, 0, 4, above).start()
        ag_copy(half, 0, 5, below).start()
        sib_copy(half, 0, core).start()
        gv_ref[:, cut] = jnp.concatenate(gvs, axis=1)
        for i in range(2):
            ubs[hs[i]] = us[i]

    raw = jnp.concatenate([raw_all[0, src_me], raw_all[1, src_me]], axis=1)

    def part(off):
        rows = pl.ds(pl.multiple_of(z_at[off] * NH * W, NH * W), NH * W)
        out = nt(raw, kw_ref[rows, :])
        for piece in range(NH):
            zs[off, piece] = out[:, piece * W:piece * W + W].astype(bf16)

    def z_far(way):
        both = pl.ds(2 * way, 2)
        return head_copy(
            zs.at[4, both], zr.at[way, 0, both], z_ss, z_rs.at[way, 0],
            z_at[2 if way == 0 else 6],
        )

    def z_copy(way, n, piece):
        off = 4 - n if way == 0 else 4 + n
        return head_copy(
            zs.at[off, piece], zr.at[way, n, piece], z_ss, z_rs.at[way, NH * n + piece],
            z_at[1 if way == 0 else 7],
        )

    def z_add(n, early, i):
        for way in range(2):
            piece = 2 * (1 - way if early else way) + i
            off = 4 - n if way == 0 else 4 + n
            z_copy(way, n - 1, piece).wait_recv()
            total = zs[off, piece].astype(f32) + zr[way, n - 1, piece].astype(f32)
            if n == 2 and not early:
                if i == 0:
                    z_far(way).wait_recv()
                total = total + zr[way, 0, piece].astype(f32)
            zs[off, piece] = total.astype(bf16)
            z_copy(way, n, piece).start()

    def relay(half):
        ag_copy(half, 3, 0, sib).wait_recv()
        ag_copy(half, 3, 2, above).start()
        ag_copy(half, 1, 1, sib).wait_recv()
        ag_copy(half, 1, 3, below).start()

    def near(half):
        ag_copy(half, 3, 4, sib).wait_recv()
        sib_copy(half, 3, core).start()
        ag_copy(half, 1, 5, sib).wait_recv()
        sib_copy(half, 1, core).start()

    def far(half):
        ag_copy(half, 2, 2, sib).wait_recv()
        ag_copy(half, 2, 3, sib).wait_recv()
        sib_copy(half, 2, core).start()

    def turn(src, c):
        cols = pl.ds(pl.multiple_of(src * W, W), W)
        for xx in range(NX):
            both = jnp.concatenate([tokcol[0, src, xx], tokcol[1, src, xx]], axis=0)
            tok_t[xx * W:xx * W + W, cols] = both.T
        return c

    x_at = [(x + i) % NX for i in range(NX)]
    right, left = dev(y, x_at[1], core), dev(y, x_at[3], core)

    def rs_copy(half, off, piece):
        rows = low if piece == 0 else high
        to_right = off == 1 or (off == 2 and piece == 0)
        return seq_copy(
            rs_s.at[half, off, rows], rs_r.at[half, off, rows], rs_ss.at[half],
            rs_rs.at[half, 2 * off + piece], right if to_right else left,
        )

    def products(half):
        for off in range(NY):
            sib_copy(half, off, 1 - core).wait_recv()
        out = mm(tok_t[...], raw_all[half].reshape(NC * NY * W, 2 * W))
        for xx in range(NX):
            psum[half, xx] = out[xx * W:xx * W + W]
        for off in (2, 1, 3):
            rs_s[half, off] = psum[half, x_at[off]].astype(bf16)
            if off == 2:
                rs_copy(half, 2, 0).start()
                rs_copy(half, 2, 1).start()
            else:
                rs_copy(half, off, 1 if off == 1 else 0).start()

    def rs_add(half):
        for off, piece in ((1, 0), (3, 1)):
            rows = slice(0, W // 2) if piece == 0 else slice(W // 2, W)
            rs_copy(half, 2, piece).wait_recv()
            rs_s[half, off, rows] = (
                psum[half, x_at[off], rows] + rs_r[half, 2, rows].astype(f32)
            ).astype(bf16)
            rs_copy(half, off, piece).start()

    def rs_end(half):
        for off in (1, 3):
            for piece in range(2):
                rs_copy(half, off, piece).wait_recv()
        gkw_ref[:, 2 * W * half:2 * W * (half + 1)] = (
            psum[half, x] + rs_r[half, 1].astype(f32) + rs_r[half, 3].astype(f32)
        )

    def grad_query(h):
        hs = slice(h * W, h * W + W)
        bi, bj = batch_of()
        g = g_ref[:, hs]
        lower = jnp.where(bi >= bj, nt(g, ubs[h]), 0.0).astype(bf16)
        gq_ref[:, hs] = (mm(g, wl[h, 0]) - rates[h] * mm(lower, kbs[h])).astype(bf16)

    part(3)
    z_copy(0, 1, 2).start()
    z_copy(0, 1, 3).start()
    part(5)
    z_copy(1, 1, 0).start()
    z_copy(1, 1, 1).start()
    part(4)
    z_far(0).start()
    z_far(1).start()
    for i in range(2):
        z_copy(0, 1, i).start()
        z_copy(1, 1, 2 + i).start()
    relay(core)
    near(core)
    part(2)
    part(6)
    relay(1 - core)
    near(1 - core)
    tz_in.wait_recv()
    lax.fori_loop(0, NC * NY, turn, 0)
    z_add(2, True, 0)
    z_add(2, True, 1)
    far(core)
    far(1 - core)
    products(core)
    z_add(2, False, 0)
    products(1 - core)
    z_add(2, False, 1)
    part(1)
    part(7)
    z_add(3, True, 0)
    z_add(3, True, 1)
    rs_add(core)
    z_add(3, False, 0)
    z_add(3, False, 1)
    rs_add(1 - core)
    part(0)
    leave[3].start()
    for h in range(NH):
        grad_query(h)
    leave[2].start()

    for piece in (2, 3, 0, 1):
        z_copy(0, 3, piece).wait_recv()
        z_copy(1, 3, piece).wait_recv()
        gt_ref[:, piece * W:piece * W + W] = (
            zs[0, piece].astype(f32) + zr[0, 3, piece].astype(f32) + zr[1, 3, piece].astype(f32)
        ).astype(bf16)
    leave[0].start()
    rs_end(0)
    rs_end(1)
    leave[1].start()

    sm_sum.wait_send()
    count(ef_recv, ef_ss, ef_rs, lambda c: c.wait_send())
    tok_sum.wait_send()
    tz_out.wait_send()
    for to_pos in range(1, NY):
        @pl.when(to_pos > pos)
        def _():
            seq_copy(tot_send, tot_recv.at[0], tot_ss.at[to_pos], tot_rs.at[0], sib).wait_send()
    count(x_in, x_ss, x_rs, lambda c: c.wait_send())
    x_out.wait_send()
    for half in range(2):
        ref = raw_all.at[half, pl.ds(0, 7)]
        seq_copy(ref, ref, ag_ss.at[half], sib_rs.at[half, 0], sib).wait_send()
        ref = rs_s.at[half, pl.ds(0, 3)]
        seq_copy(ref, ref, rs_ss.at[half], rs_rs.at[half, 0], sib).wait_send()
    some_z = zs.at[pl.ds(0, 7)]
    head_copy(some_z, some_z, z_ss, z_rs.at[0, 0], z_at[1]).wait_send()
    for copy in leave:
        copy.wait()


def hand_over(a0, a1, a2, a3, b0, b1, b2, b3, v0, v1, v2, v3, sems):
    ins = [
        pltpu.make_async_copy(a, v, sems.at[i])
        for i, (a, v) in enumerate(((a0, v0), (a1, v1), (a2, v2), (a3, v3)))
    ]
    outs = [
        pltpu.make_async_copy(v, b, sems.at[4 + i])
        for i, (v, b) in enumerate(((v0, b0), (v1, b1), (v2, b2), (v3, b3)))
    ]
    for copy in ins:
        copy.start()
    for copy, after in zip(ins, outs):
        copy.wait()
        after.start()
    for copy in outs:
        copy.wait()


def per_device(tokens, key_weight, queries, values, grad_out, inner_start, head_rate):
    vmem = pl.BlockSpec(memory_space=pltpu.VMEM)
    smem = pl.BlockSpec(memory_space=pltpu.SMEM)
    anywhere = pl.BlockSpec(memory_space=pl.ANY)
    cols = NH * W
    sem = pltpu.SemaphoreType.DMA
    shapes = (
        jax.ShapeDtypeStruct((W, cols), bf16),
        jax.ShapeDtypeStruct((W, cols), f32),
        jax.ShapeDtypeStruct((W, cols), bf16),
        jax.ShapeDtypeStruct((W, cols), bf16),
    )
    outs = pl.pallas_call(
        kernel,
        out_shape=shapes,
        in_specs=[anywhere] * 6 + [smem],
        out_specs=(anywhere,) * 4,
        scratch_shapes=[
            *[pltpu.VMEM(a.shape, a.dtype) for a in shapes],
            pltpu.VMEM(tokens.shape, bf16),
            pltpu.VMEM(key_weight.shape, bf16),
            pltpu.VMEM((W, cols), bf16),
            pltpu.VMEM((W, cols), bf16),
            pltpu.VMEM((W, cols), bf16),
            pltpu.VMEM((NH, W, W), f32),
            pltpu.VMEM((W, cols), f32),
            pltpu.VMEM((2, NC * NY, NX, W // 2, W), bf16),
            pltpu.VMEM((NX * W, NC * NY * W), bf16),
            pltpu.VMEM((NH, 2, 2 * W, W), bf16),
            pltpu.VMEM((2, 2, 2 * W, W), bf16),
            pltpu.VMEM((2, 2, 2 * W, W), bf16),
            pltpu.VMEM((2, 2, 2 * W, W), bf16),
            pltpu.VMEM((NX, 2 * W, W), bf16),
            pltpu.VMEM((2 * W, W), bf16),
            pltpu.VMEM((NY, 2 * W, W), bf16),
            pltpu.VMEM((2, 2 * W, W), f32),
            pltpu.VMEM((W, W), f32),
            pltpu.VMEM((NX, W, W), bf16),
            pltpu.VMEM((4, W, W), bf16),
            pltpu.VMEM((2, 2, W, W), bf16),
            pltpu.VMEM((NH, 2, W, W), bf16),
            pltpu.VMEM((NH, W, W), f32),
            pltpu.VMEM((NH, W, W), f32),
            pltpu.VMEM((NH, W, W), bf16),
            pltpu.VMEM((NH, W, W), bf16),
            pltpu.VMEM((NH, W, W), f32),
            pltpu.VMEM((NH, W, W), bf16),
            pltpu.VMEM((NH, W, W), f32),
            pltpu.VMEM((NH, W, W), bf16),
            pltpu.VMEM((2, NC * NY, W, 2 * W), bf16),
            pltpu.VMEM((2, NX, W, 2 * W), f32),
            pltpu.VMEM((2, NX, W, 2 * W), bf16),
            pltpu.VMEM((2, NX, W, 2 * W), bf16),
            pltpu.VMEM((NZ, NH, W, W), bf16),
            pltpu.VMEM((2, 4, NH, W, W), bf16),
            sem((5 + KW_PARTS,)),
            sem((4,)),
            sem, sem, sem, sem,
            sem, sem, sem, sem,
            sem((NY,)), sem((NY,)),
            sem, sem, sem, sem,
            sem((2,)), sem((2, 6)), sem((2, 4)),
            sem((2,)), sem((2, 8)),
            sem, sem((2, 4 * NH)),
        ],
        compiler_params=pltpu.CompilerParams(
            collective_id=0, has_side_effects=True, vmem_limit_bytes=56 * 1024 * 1024
        ),
        name="layer",
    )(tokens, key_weight, queries, values, grad_out, inner_start, head_rate)
    return pl.pallas_call(
        hand_over,
        out_shape=shapes,
        in_specs=[anywhere] * 4,
        out_specs=(anywhere,) * 4,
        scratch_shapes=[pltpu.VMEM(a.shape, a.dtype) for a in shapes] + [sem((8,))],
        name="hand_over",
    )(*outs)


def solution(mesh):
    placed = (
        P("seq", None),
        P(None, "head"),
        P("seq", "head"),
        P("seq", "head"),
        P("seq", "head"),
        P("head", None, None),
        P("head"),
    )
    return jax.shard_map(
        per_device,
        mesh=mesh,
        in_specs=placed,
        out_specs=(P("seq", "head"),) * 4,
        check_vma=False,
    )
```
